32 devices in a mesh: rows: 4 (over z), cols: 8 (over y, x, core).
Axes of the slice: x: 2, y: 2, z: 4, core: 2. Of those that a mesh axis runs over, the one named last changes fastest.
Arguments:
- embeddings: bfloat16 [229376, 1024], P(('rows', 'cols'))
- factor_cols: bfloat16 [229376, 512], P(('rows', 'cols')), may hold values from -0.12 to 0.12, as said below
- solved: int32 [229376], P(('rows', 'cols')), may hold values from 0 to 16
- pivots: int32 [256], replicated, may hold values from 0 to 229375, as said below
Outputs:
- new_cols: bfloat16 [229376, 256], P(('rows', 'cols'))
- gains: float32 [229376], P(('rows', 'cols'))
- best_gain: float32 [], replicated
The draws below stay inside these ranges and needn't reach their ends.
Inputs may be any that keep to these rules, and one draw needn't show every extreme that they name: `pivots`: 256 distinct row numbers in increasing order; the 7168 consecutive rows of one device hold at most 16 of them, and some device holds exactly 16. `factor_cols`: the pivots' factor rows F satisfy: every eigenvalue of F F^T is below 1.
All inputs are finite; a program needn't handle non-finite values.
Results may differ from the reference program's by a relative error of at most 0.001.
Values may be sent and summed in bfloat16 or wider, within the bound.
A program may use at most 128 MiB of HBM per device.

```python
import jax
import jax.numpy as jnp
from jax import lax

D = 1024
K0 = 512
P_SIZE = 256
PMAX = 16
ROWS_DEV = 7168
NUM_ROWS = 229376


def draw_embeddings(key, part):
    base = jax.random.fold_in(key, 11)
    k_noise, k_shared, k_amp = jax.random.split(base, 3)
    shared = jax.random.normal(k_shared, (D,), jnp.float32)
    noise = jax.random.normal(k_noise, (NUM_ROWS, D), jnp.float32)
    amp = jax.random.uniform(k_amp, (NUM_ROWS, 1), jnp.float32, 0.5, 2.0)
    return (noise + amp * shared[None, :]).astype(jnp.bfloat16)


def draw_factor_cols(key, part):
    base = jax.random.fold_in(key, 37)
    k_noise = jax.random.fold_in(base, 0)
    values = jnp.clip(0.02 * jax.random.normal(k_noise, (NUM_ROWS, K0), jnp.float32), -0.12, 0.12)
    return values.astype(jnp.bfloat16)


def draw_pivots(key, part):
    base = jax.random.fold_in(key, 23)
    devices = NUM_ROWS // ROWS_DEV
    k_heavy, k_perm, k_offset = jax.random.split(base, 3)
    heavy = jax.random.randint(k_heavy, (), 0, devices).astype(jnp.int32)
    others = jax.random.permutation(k_perm, (devices - 1) * PMAX)[:P_SIZE - PMAX].astype(jnp.int32)
    owner = others // PMAX
    owner = owner + (owner >= heavy).astype(jnp.int32)
    slot_other = owner * PMAX + others % PMAX
    slot_heavy = heavy * PMAX + jnp.arange(PMAX, dtype=jnp.int32)
    slots = jnp.sort(jnp.concatenate([slot_heavy, slot_other]))
    spacing = ROWS_DEV // PMAX
    offset = jax.random.randint(k_offset, (P_SIZE,), 0, spacing).astype(jnp.int32)
    return (slots // PMAX * ROWS_DEV + slots % PMAX * spacing + offset).astype(jnp.int32)


def place_ends(values, stream_key, least, high):
    longest = values.shape.index(max(values.shape))
    spots = []
    for shift in (0, 1):
        where = [jax.random.randint(jax.random.fold_in(stream_key, axis), (), 0, length) for axis, length in enumerate(values.shape)]
        where[longest] = (where[longest] + shift) % values.shape[longest]
        spots.append(tuple(where))
    return values.at[spots[0]].set(least).at[spots[1]].set(high)


def setup_inputs(seed: int = 0) -> dict:
    key_list = jax.random.split(jax.random.key(seed), 5)
    return {
        "embeddings": draw_embeddings(jax.random.fold_in(key_list[4], 71), 0),
        "factor_cols": draw_factor_cols(jax.random.fold_in(key_list[4], 71), 0),
        "solved": place_ends(jax.random.randint(key_list[2], (NUM_ROWS,), 0, 17), jax.random.fold_in(key_list[2], 1), 0, 16).astype(jnp.int32),
        "pivots": draw_pivots(jax.random.fold_in(key_list[4], 71), 0),
    }


EPS = 1e-06
TAU = 6.0
RIDGE = 1.0

def learn(counts):
    c = counts.astype(jnp.float32)
    return (c * (16.0 - c) + 8.0) / 72.0

def scales(emb):
    x = emb.astype(jnp.float32)
    return jnp.sqrt(lax.optimization_barrier(jnp.mean(x * x, axis=1)) + EPS)

def kernel_panel(left_emb, left_fac, left_q, left_norm, left_ids, piv_emb, piv_fac, piv_q, piv_norm, pivots):
    dims = (((1,), (1,)), ((), ()))
    dots = lax.dot_general(left_emb.astype(jnp.float32), piv_emb.astype(jnp.float32), dims, preferred_element_type=jnp.float32)
    width = left_emb.shape[1] * 1.0
    cosine = dots / (width * left_norm[:, None] * piv_norm[None, :])
    similar = jnp.exp(TAU * (cosine - 1.0))
    ridge = jnp.where(left_ids[:, None] == pivots[None, :], RIDGE, 0.0)
    shared = lax.dot_general(left_fac.astype(jnp.float32), piv_fac.astype(jnp.float32), dims, preferred_element_type=jnp.float32)
    return left_q[:, None] * piv_q[None, :] * similar + ridge - shared

def reference(embeddings, factor_cols, solved, pivots):
    piv_emb = embeddings[pivots]
    piv_fac = factor_cols[pivots]
    piv_q = learn(solved[pivots])
    piv_norm = scales(piv_emb)
    block = kernel_panel(piv_emb, piv_fac, piv_q, piv_norm, pivots, piv_emb, piv_fac, piv_q, piv_norm, pivots)
    lower = jnp.linalg.cholesky(block)
    blocks = embeddings.shape[0] // ROWS_DEV

    def one(index):
        start = index * ROWS_DEV
        emb = lax.dynamic_slice_in_dim(embeddings, start, ROWS_DEV, 0)
        fac = lax.dynamic_slice_in_dim(factor_cols, start, ROWS_DEV, 0)
        counts = lax.dynamic_slice_in_dim(solved, start, ROWS_DEV, 0)
        row_q = learn(counts)
        row_ids = start + jnp.arange(ROWS_DEV, dtype=jnp.int32)
        panel = kernel_panel(emb, fac, row_q, scales(emb), row_ids, piv_emb, piv_fac, piv_q, piv_norm, pivots)
        full = jax.scipy.linalg.solve_triangular(lower, panel.T, lower=True).T
        facf = fac.astype(jnp.float32)
        gain = row_q * row_q + RIDGE - lax.optimization_barrier(jnp.sum(facf * facf, axis=1)) - lax.optimization_barrier(jnp.sum(full * full, axis=1))
        return (full.astype(jnp.bfloat16), gain)
    new_cols, gains = lax.map(one, jnp.arange(blocks, dtype=jnp.int32))
    new_cols = new_cols.reshape(blocks * ROWS_DEV, pivots.shape[0])
    gains = gains.reshape(blocks * ROWS_DEV)
    return (new_cols, gains, jnp.max(gains))
```

```python
import functools

import jax
import jax.numpy as jnp
from jax import lax
from jax.experimental import pallas as pl
from jax.experimental.pallas import tpu as pltpu
from jax.sharding import PartitionSpec as P

PMAX = 16
EPS = 1e-06
TAU = 6.0
RIDGE = 1.0
LANES = 128
GROUP = 8
TILE = 1024
SUB = 256
VMEM_LIMIT = 56 * 1024 * 1024
MESH = pl.DeviceIdType.MESH
NT = (((1,), (1,)), ((), ()))


def learn(counts):
    c = counts.astype(jnp.float32)
    return (c * (16.0 - c) + 8.0) / 72.0


def pick_kernel(n_cols, piv_ref, solved_ref, emb_ref, fac_ref, out_ref, ebuf, fbuf, sem):
    rows_here, width = emb_ref.shape
    fac_width = fac_ref.shape[1]
    total = piv_ref.shape[0]
    first = (lax.axis_index("rows") * n_cols + lax.axis_index("cols")) * rows_here
    before = jnp.int32(0)
    step = 1
    while step * 2 <= total:
        step *= 2
    while step:
        probe = jnp.minimum(before + step - 1, total - 1)
        inside = before + step <= total
        before = before + jnp.where(inside & (piv_ref[probe] < first), step, 0)
        step //= 2
    copies = []
    spots = []
    for r in range(PMAX):
        idx = jnp.clip(piv_ref[jnp.minimum(before + r, total - 1)] - first, 0, rows_here - 1)
        base = pl.multiple_of(lax.shift_left(lax.shift_right_logical(idx, 4), 4), 16)
        for src, dst, k in ((emb_ref, ebuf, 0), (fac_ref, fbuf, 1)):
            copy = pltpu.make_async_copy(
                src.at[pl.ds(base, 16), :], dst.at[pl.ds(16 * r, 16), :], sem.at[k, r]
            )
            copy.start()
            copies.append(copy)
        spots.append((idx, idx - base + 16 * r))
    row = lax.broadcasted_iota(jnp.int32, (PMAX, 16 * PMAX), 0)
    lane = lax.broadcasted_iota(jnp.int32, (PMAX, 16 * PMAX), 1)
    row1 = lax.broadcasted_iota(jnp.int32, (PMAX, LANES), 0)
    want = jnp.zeros((PMAX, 16 * PMAX), jnp.int32)
    count = jnp.zeros((PMAX, LANES), jnp.int32)
    for r, (idx, spot) in enumerate(spots):
        want = jnp.where(row == r, spot, want)
        count = jnp.where(row1 == r, solved_ref[idx], count)
    pick = jnp.where(lane == want, 1.0, 0.0).astype(jnp.bfloat16)
    out_ref[:, width + fac_width:] = count.astype(jnp.float32).astype(jnp.bfloat16)
    for copy in copies:
        copy.wait()
    out_ref[:, :width] = jnp.dot(
        pick, ebuf[...], preferred_element_type=jnp.float32
    ).astype(jnp.bfloat16)
    out_ref[:, width:width + fac_width] = jnp.dot(
        pick, fbuf[...], preferred_element_type=jnp.float32
    ).astype(jnp.bfloat16)


def gather_kernel(n_rows, n_cols, own_ref, out_ref, send_sem, recv_sem, own_sem):
    r = lax.axis_index("rows")
    c = lax.axis_index("cols")
    pairs = n_cols // 2
    h = c // 2
    k = c - 2 * h
    twin = 2 * h + 1 - k

    def other_row(j):
        return lax.rem(r + j, n_rows)

    def other_col(i):
        return 2 * lax.rem(h + i, pairs) + k

    barrier = pltpu.get_barrier_semaphore()
    peers = [(other_row(j), c) for j in range(1, n_rows)]
    peers += [(r, other_col(i)) for i in range(1, pairs)]
    peers.append((r, twin))
    for peer in peers:
        pl.semaphore_signal(barrier, inc=1, device_id=peer, device_id_type=MESH)
    own = pltpu.make_async_copy(own_ref, out_ref.at[r * n_cols + c], own_sem)
    own.start()
    pl.semaphore_wait(barrier, len(peers))

    sent = []

    def send(src, block, peer):
        copy = pltpu.make_async_remote_copy(
            src_ref=src,
            dst_ref=out_ref.at[block],
            send_sem=send_sem.at[len(sent)],
            recv_sem=recv_sem.at[block],
            device_id=peer,
            device_id_type=MESH,
        )
        copy.start()
        sent.append(copy)

    def arrived(block):
        pltpu.make_async_remote_copy(
            src_ref=own_ref,
            dst_ref=out_ref.at[block],
            send_sem=send_sem.at[0],
            recv_sem=recv_sem.at[block],
            device_id=(r, twin),
            device_id_type=MESH,
        ).wait_recv()

    me = r * n_cols + c
    for i in range(1, pairs):
        send(own_ref, me, (r, other_col(i)))
    for j in range(1, n_rows):
        send(own_ref, me, (other_row(j), c))
    send(own_ref, me, (r, twin))
    order = [j for j in range(1, n_rows)]
    for j in order:
        block = other_row(j) * n_cols + c
        arrived(block)
        for i in range(1, pairs):
            send(out_ref.at[block], block, (r, other_col(i)))
        send(out_ref.at[block], block, (r, twin))
    for j in [0] + order:
        for i in range(1, pairs):
            block = other_row(j) * n_cols + other_col(i)
            arrived(block)
            send(out_ref.at[block], block, (r, twin))
    for j in range(n_rows):
        for i in range(pairs):
            arrived(other_row(j) * n_cols + 2 * lax.rem(h + i, pairs) + 1 - k)
    own.wait()
    for copy in sent:
        copy.wait_send()


def split(x):
    hi = x.astype(jnp.bfloat16)
    return hi, (x - hi.astype(jnp.float32)).astype(jnp.bfloat16)


def factor_kernel(
    rows_here, width, fac_width, piv_ref, all_ref, out_ref, hi_ref, lo_ref, side_ref, work
):
    total = piv_ref.shape[1]
    slots = all_ref.shape[0]
    f32 = jnp.float32
    sub = lax.broadcasted_iota(jnp.int32, (total, total), 0)
    lane = lax.broadcasted_iota(jnp.int32, (total, total), 1)
    eye = sub == lane
    ids = jnp.broadcast_to(piv_ref[...].astype(f32), (total, total))
    ids = jnp.sum(jnp.where(eye, ids, 0.0), axis=1, keepdims=True)
    place = lax.broadcasted_iota(jnp.int32, (total, slots), 0)
    slot = lax.broadcasted_iota(jnp.int32, (total, slots), 1)
    owner = lax.shift_right_logical(slot, PMAX.bit_length() - 1)
    low = (owner * rows_here).astype(f32)
    above = ids >= low
    before = total - jnp.sum(jnp.where(above, 1.0, 0.0), axis=0, keepdims=True)
    rank = place.astype(f32) - before
    chosen = above & (ids < low + rows_here) & (rank == (slot - owner * PMAX).astype(f32))
    chosen = jnp.where(chosen, 1.0, 0.0).astype(jnp.bfloat16)
    full_width = all_ref.shape[1]
    part = width // 2
    for start in range(0, full_width, part):
        size = min(part, full_width - start)
        out_ref[:, start:start + size] = jnp.dot(
            chosen, all_ref[:, start:start + size], preferred_element_type=f32
        ).astype(jnp.bfloat16)
    emb = out_ref[:, :width]
    fac = out_ref[:, width:width + fac_width]
    count = out_ref[:, width + fac_width:width + fac_width + 1].astype(f32)
    wide = emb.astype(f32)
    norm = lax.rsqrt(jnp.sum(wide * wide, axis=1, keepdims=True) / width + EPS)
    q = learn(count)

    def to_row(col):
        return jnp.sum(jnp.where(eye, col, 0.0), axis=0, keepdims=True)

    norm_row = to_row(norm) * (TAU / width)
    q_row = to_row(q)
    side_ref[0:1, :] = norm_row
    side_ref[1:2, :] = q_row
    dots = lax.dot_general(emb, emb, NT, preferred_element_type=f32)
    shared = lax.dot_general(fac, fac, NT, preferred_element_type=f32)
    block = q * q_row * jnp.exp(dots * norm * norm_row - TAU) - shared
    work[...] = block + jnp.where(eye, RIDGE, 0.0)

    row8 = lax.broadcasted_iota(jnp.int32, (GROUP, total), 0)
    lane8 = lax.broadcasted_iota(jnp.int32, (GROUP, total), 1)

    def step(b, carry):
        start = pl.multiple_of(b * GROUP, GROUP)
        rows = work[pl.ds(start, GROUP), :]
        cols = [
            jnp.broadcast_to(
                jnp.sum(jnp.where(lane8 == start + i, rows, 0.0), axis=1, keepdims=True),
                (GROUP, total),
            )
            for i in range(GROUP)
        ]
        left = jnp.where(lane8 >= start + GROUP, rows, 0.0)
        solved = jnp.where(
            (lane8 >= start) & (lane8 < start + GROUP),
            jnp.where(lane8 == start + row8, 1.0, 0.0),
            rows,
        )
        diag = jnp.ones((GROUP, total), f32)
        for i in range(GROUP):
            d = cols[i][i:i + 1, :]
            diag = jnp.where(row8 == i, d, diag)
            m = jnp.where(row8 > i, cols[i] * (1.0 / d), 0.0)
            for n in range(i + 1, GROUP):
                cols[n] = cols[n] - m * cols[n][i:i + 1, :]
            solved = solved - m * solved[i:i + 1, :]
            left = left - m * left[i:i + 1, :]
        scale = lax.rsqrt(diag)
        solved = solved * scale
        left = left * scale
        delta = lax.dot_general(
            left, solved, (((0,), (0,)), ((), ())),
            precision=lax.Precision.HIGHEST, preferred_element_type=f32,
        )
        keep = jnp.where((lane >= start) & (lane < start + GROUP), 0.0, work[...])
        work[...] = keep - delta
        work[pl.ds(start, GROUP), :] = solved
        return carry

    lax.fori_loop(0, total // GROUP, step, 0)
    hi, lo = split(work[...])
    hi_ref[...] = hi
    lo_ref[...] = lo


def panel_kernel(
    n_cols, rows_here, width, fac_width,
    emb_ref, fac_ref, solved_ref, piv_ref, ids_ref, hi_ref, lo_ref, side_ref,
    new_ref, gain_ref, best_ref,
):
    f32 = jnp.float32
    total = ids_ref.shape[1]
    tile = emb_ref.shape[0]
    step = pl.program_id(0)
    first = (lax.axis_index("rows") * n_cols + lax.axis_index("cols")) * rows_here + step * tile
    piv_emb = piv_ref[:, :width]
    piv_fac = piv_ref[:, width:width + fac_width]
    hi_w = hi_ref[...]
    lo_w = lo_ref[...]
    norm_row = side_ref[0:1, :]
    q_row = side_ref[1:2, :]
    ids = ids_ref[...] - first
    sub = lax.broadcasted_iota(jnp.int32, (LANES, LANES), 0)
    lane = lax.broadcasted_iota(jnp.int32, (LANES, LANES), 1)
    eye = sub == lane
    row = lax.broadcasted_iota(jnp.int32, (SUB, total), 0)
    q_lanes = learn(solved_ref[...])
    best = jnp.full((1, LANES), -jnp.inf, f32)
    for s in range(0, tile, SUB):
        emb = emb_ref[s:s + SUB, :]
        fac = fac_ref[s:s + SUB, :]
        dots = lax.dot_general(emb, piv_emb, NT, preferred_element_type=f32)
        shared = lax.dot_general(fac, piv_fac, NT, preferred_element_type=f32)
        wide = emb.astype(f32)
        norm = lax.rsqrt(jnp.sum(wide * wide, axis=1, keepdims=True) / width + EPS)
        widef = fac.astype(f32)
        used = jnp.sum(widef * widef, axis=1, keepdims=True)
        q = jnp.concatenate(
            [
                jnp.sum(
                    jnp.where(eye, q_lanes[g:g + 1, :], 0.0), axis=1, keepdims=True
                )
                for g in range(s // LANES, (s + SUB) // LANES)
            ],
            axis=0,
        )
        panel = q * q_row * jnp.exp(dots * norm * norm_row - TAU) - shared
        panel = jnp.where(row + s == ids, panel + RIDGE, panel)
        hi, lo = split(panel)
        full = (
            lax.dot_general(hi, hi_w, NT, preferred_element_type=f32)
            + lax.dot_general(hi, lo_w, NT, preferred_element_type=f32)
            + lax.dot_general(lo, hi_w, NT, preferred_element_type=f32)
        )
        new_ref[s:s + SUB, :] = full.astype(jnp.bfloat16)
        gain = q * q + RIDGE - used - jnp.sum(full * full, axis=1, keepdims=True)
        for g in range(0, SUB, LANES):
            line = jnp.sum(jnp.where(eye, gain[g:g + LANES, :], 0.0), axis=0, keepdims=True)
            at = (s + g) // LANES
            gain_ref[at:at + 1, :] = line
            best = jnp.maximum(best, line)
    best = jnp.broadcast_to(best, best_ref.shape)

    @pl.when(step == 0)
    def _():
        best_ref[...] = best

    @pl.when(step > 0)
    def _():
        best_ref[...] = jnp.maximum(best_ref[...], best)


def best_kernel(n_rows, n_cols, own_ref, out_ref, stage, buf_r, buf_c, send_r, recv_r, send_c, recv_c):
    r = lax.axis_index("rows")
    c = lax.axis_index("cols")
    barrier = pltpu.get_barrier_semaphore()
    peers_r = [(lax.rem(r + j, n_rows), c) for j in range(1, n_rows)]
    peers_c = [(r, lax.rem(c + i, n_cols)) for i in range(1, n_cols)]
    for peer in peers_r + peers_c:
        pl.semaphore_signal(barrier, inc=1, device_id=peer, device_id_type=MESH)
    pl.semaphore_wait(barrier, len(peers_r) + len(peers_c))

    def exchange(src, buf, send_sem, recv_sem, peers):
        copies = []
        for j, peer in enumerate(peers):
            copy = pltpu.make_async_remote_copy(
                src_ref=src, dst_ref=buf.at[j], send_sem=send_sem.at[j],
                recv_sem=recv_sem.at[j], device_id=peer, device_id_type=MESH,
            )
            copy.start()
            copies.append(copy)
        top = src[...]
        for j, copy in enumerate(copies):
            copy.wait_recv()
            top = jnp.maximum(top, buf[j])
        for copy in copies:
            copy.wait_send()
        return top

    stage[...] = exchange(own_ref, buf_r, send_r, recv_r, peers_r)
    out_ref[0, 0] = jnp.max(exchange(stage, buf_c, send_c, recv_c, peers_c))


def body(n_rows, n_cols, embeddings, factor_cols, solved, pivots):
    rows_here, width = embeddings.shape
    fac_width = factor_cols.shape[1]
    total = pivots.shape[0]
    devices = n_rows * n_cols
    packet = width + fac_width + LANES
    bf16 = jnp.bfloat16
    vmem = pl.BlockSpec(memory_space=pltpu.VMEM)
    smem = pl.BlockSpec(memory_space=pltpu.SMEM)
    params = functools.partial(pltpu.CompilerParams, vmem_limit_bytes=VMEM_LIMIT)
    own = pl.pallas_call(
        functools.partial(pick_kernel, n_cols),
        out_shape=jax.ShapeDtypeStruct((PMAX, packet), bf16),
        in_specs=[smem, smem, pl.BlockSpec(memory_space=pl.ANY), pl.BlockSpec(memory_space=pl.ANY)],
        out_specs=vmem,
        scratch_shapes=[
            pltpu.VMEM((16 * PMAX, width), bf16),
            pltpu.VMEM((16 * PMAX, fac_width), bf16),
            pltpu.SemaphoreType.DMA((2, PMAX)),
        ],
        compiler_params=params(),
        name="pick",
    )(pivots, solved, embeddings, factor_cols)
    everyone = pl.pallas_call(
        functools.partial(gather_kernel, n_rows, n_cols),
        out_shape=jax.ShapeDtypeStruct((devices, PMAX, packet), bf16),
        in_specs=[vmem],
        out_specs=vmem,
        scratch_shapes=[
            pltpu.SemaphoreType.DMA((devices,)),
            pltpu.SemaphoreType.DMA((devices,)),
            pltpu.SemaphoreType.DMA,
        ],
        compiler_params=params(collective_id=0, has_side_effects=True),
        name="gather",
    )(own)
    ids = pivots.reshape(1, total)
    piv, hi, lo, side = pl.pallas_call(
        functools.partial(factor_kernel, rows_here, width, fac_width),
        out_shape=[
            jax.ShapeDtypeStruct((total, packet), bf16),
            jax.ShapeDtypeStruct((total, total), bf16),
            jax.ShapeDtypeStruct((total, total), bf16),
            jax.ShapeDtypeStruct((8, total), jnp.float32),
        ],
        in_specs=[vmem, vmem],
        out_specs=[vmem] * 4,
        scratch_shapes=[pltpu.VMEM((total, total), jnp.float32)],
        compiler_params=params(),
        name="factor",
    )(ids, everyone.reshape(devices * PMAX, packet))
    tile = TILE
    lines = rows_here // LANES

    def whole(shape):
        return pl.BlockSpec(shape, lambda t: (0, 0))

    new_cols, gains, best = pl.pallas_call(
        functools.partial(panel_kernel, n_cols, rows_here, width, fac_width),
        out_shape=[
            jax.ShapeDtypeStruct((rows_here, total), bf16),
            jax.ShapeDtypeStruct((lines, LANES), jnp.float32),
            jax.ShapeDtypeStruct((8, LANES), jnp.float32),
        ],
        grid=(rows_here // tile,),
        in_specs=[
            pl.BlockSpec((tile, width), lambda t: (t, 0)),
            pl.BlockSpec((tile, fac_width), lambda t: (t, 0)),
            pl.BlockSpec((tile // LANES, LANES), lambda t: (t, 0)),
            whole((total, packet)),
            whole((1, total)),
            whole((total, total)),
            whole((total, total)),
            whole((8, total)),
        ],
        out_specs=[
            pl.BlockSpec((tile, total), lambda t: (t, 0)),
            pl.BlockSpec((tile // LANES, LANES), lambda t: (t, 0)),
            whole((8, LANES)),
        ],
        compiler_params=params(),
        name="panel",
    )(embeddings, factor_cols, solved.reshape(lines, LANES), piv, ids, hi, lo, side)
    top = pl.pallas_call(
        functools.partial(best_kernel, n_rows, n_cols),
        out_shape=jax.ShapeDtypeStruct((1, 1), jnp.float32),
        in_specs=[vmem],
        out_specs=smem,
        scratch_shapes=[
            pltpu.VMEM((8, LANES), jnp.float32),
            pltpu.VMEM((n_rows, 8, LANES), jnp.float32),
            pltpu.VMEM((n_cols, 8, LANES), jnp.float32),
            pltpu.SemaphoreType.DMA((n_rows,)),
            pltpu.SemaphoreType.DMA((n_rows,)),
            pltpu.SemaphoreType.DMA((n_cols,)),
            pltpu.SemaphoreType.DMA((n_cols,)),
        ],
        compiler_params=params(collective_id=1, has_side_effects=True),
        name="best",
    )(best)
    return new_cols, gains.reshape(rows_here), top.reshape(())


def solution(mesh):
    n_rows, n_cols = mesh.shape["rows"], mesh.shape["cols"]
    in_specs = (P(("rows", "cols"), None), P(("rows", "cols"), None), P(("rows", "cols")), P())
    out_specs = (P(("rows", "cols"), None), P(("rows", "cols")), P())
    return jax.shard_map(
        functools.partial(body, n_rows, n_cols),
        mesh=mesh, in_specs=in_specs, out_specs=out_specs, check_vma=False,
    )
```

```python
import functools

import jax
import jax.numpy as jnp
from jax import lax
from jax.experimental import pallas as pl
from jax.experimental.pallas import tpu as pltpu
from jax.sharding import PartitionSpec as P

PMAX = 16
EPS = 1e-06
TAU = 6.0
RIDGE = 1.0
LOG2E = 1.4426950408889634
LANES = 128
GROUP = 8
SUB = 256
VMEM_LIMIT = 56 * 1024 * 1024
MESH = pl.DeviceIdType.MESH
NT = (((1,), (1,)), ((), ()))


def learn(counts):
    c = counts.astype(jnp.float32)
    return (c * (16.0 - c) + 8.0) / 72.0


def pick_kernel(n_cols, piv_ref, solved_ref, emb_ref, fac_ref, out_ref, ebuf, fbuf, sem):
    rows_here, width = emb_ref.shape
    fac_width = fac_ref.shape[1]
    total = piv_ref.shape[0]
    first = (lax.axis_index("rows") * n_cols + lax.axis_index("cols")) * rows_here
    before = jnp.int32(0)
    step = 1
    while step * 2 <= total:
        step *= 2
    while step:
        probe = jnp.minimum(before + step - 1, total - 1)
        inside = before + step <= total
        before = before + jnp.where(inside & (piv_ref[probe] < first), step, 0)
        step //= 2
    copies = []
    spots = []
    for r in range(PMAX):
        idx = jnp.clip(piv_ref[jnp.minimum(before + r, total - 1)] - first, 0, rows_here - 1)
        base = pl.multiple_of(lax.shift_left(lax.shift_right_logical(idx, 4), 4), 16)
        for src, dst, k in ((emb_ref, ebuf, 0), (fac_ref, fbuf, 1)):
            copy = pltpu.make_async_copy(
                src.at[pl.ds(base, 16), :], dst.at[pl.ds(16 * r, 16), :], sem.at[k, r]
            )
            copy.start()
            copies.append(copy)
        spots.append((idx, idx - base + 16 * r))
    row = lax.broadcasted_iota(jnp.int32, (PMAX, 16 * PMAX), 0)
    lane = lax.broadcasted_iota(jnp.int32, (PMAX, 16 * PMAX), 1)
    row1 = lax.broadcasted_iota(jnp.int32, (PMAX, LANES), 0)
    want = jnp.zeros((PMAX, 16 * PMAX), jnp.int32)
    count = jnp.zeros((PMAX, LANES), jnp.int32)
    for r, (idx, spot) in enumerate(spots):
        want = jnp.where(row == r, spot, want)
        count = jnp.where(row1 == r, solved_ref[idx], count)
    pick = jnp.where(lane == want, 1.0, 0.0).astype(jnp.bfloat16)
    out_ref[:, width + fac_width:] = count.astype(jnp.float32).astype(jnp.bfloat16)
    for copy in copies:
        copy.wait()
    out_ref[:, :width] = jnp.dot(
        pick, ebuf[...], preferred_element_type=jnp.float32
    ).astype(jnp.bfloat16)
    out_ref[:, width:width + fac_width] = jnp.dot(
        pick, fbuf[...], preferred_element_type=jnp.float32
    ).astype(jnp.bfloat16)


def gather_kernel(n_rows, n_cols, own_ref, out_ref, send_sem, recv_sem, own_sem):
    r = lax.axis_index("rows")
    c = lax.axis_index("cols")
    pairs = n_cols // 2
    h = c // 2
    k = c - 2 * h
    twin = 2 * h + 1 - k

    def other_row(j):
        return lax.rem(r + j, n_rows)

    def other_col(i):
        return 2 * lax.rem(h + i, pairs) + k

    barrier = pltpu.get_barrier_semaphore()
    peers = [(other_row(j), c) for j in range(1, n_rows)]
    peers += [(r, other_col(i)) for i in range(1, pairs)]
    peers.append((r, twin))
    for peer in peers:
        pl.semaphore_signal(barrier, inc=1, device_id=peer, device_id_type=MESH)
    own = pltpu.make_async_copy(own_ref, out_ref.at[r * n_cols + c], own_sem)
    own.start()
    pl.semaphore_wait(barrier, len(peers))

    sent = []

    def send(src, block, peer):
        copy = pltpu.make_async_remote_copy(
            src_ref=src,
            dst_ref=out_ref.at[block],
            send_sem=send_sem.at[len(sent)],
            recv_sem=recv_sem.at[block],
            device_id=peer,
            device_id_type=MESH,
        )
        copy.start()
        sent.append(copy)

    def arrived(block):
        pltpu.make_async_remote_copy(
            src_ref=own_ref,
            dst_ref=out_ref.at[block],
            send_sem=send_sem.at[0],
            recv_sem=recv_sem.at[block],
            device_id=(r, twin),
            device_id_type=MESH,
        ).wait_recv()

    me = r * n_cols + c
    for i in range(1, pairs):
        send(own_ref, me, (r, other_col(i)))
    for j in range(1, n_rows):
        send(own_ref, me, (other_row(j), c))
    send(own_ref, me, (r, twin))
    order = [j for j in range(1, n_rows)]
    for j in order:
        block = other_row(j) * n_cols + c
        arrived(block)
        for i in range(1, pairs):
            send(out_ref.at[block], block, (r, other_col(i)))
        send(out_ref.at[block], block, (r, twin))
    for j in [0] + order:
        for i in range(1, pairs):
            block = other_row(j) * n_cols + other_col(i)
            arrived(block)
            send(out_ref.at[block], block, (r, twin))
    for j in range(n_rows):
        for i in range(pairs):
            arrived(other_row(j) * n_cols + 2 * lax.rem(h + i, pairs) + 1 - k)
    own.wait()
    for copy in sent:
        copy.wait_send()


def split(x):
    hi = x.astype(jnp.bfloat16)
    return hi, (x - hi.astype(jnp.float32)).astype(jnp.bfloat16)


def main_kernel(
    n_cols, piv_ref, all_ref, solved_ref, emb_ref, fac_ref,
    new_ref, gain_ref, best_ref,
    emb_buf, fac_buf, hi_buf, lo_buf, new_buf, piv_buf, work, in_sem, out_sem,
):
    f32, bf16 = jnp.float32, jnp.bfloat16
    rows_here, width = emb_ref.shape
    fac_width = fac_ref.shape[1]
    total = piv_ref.shape[1]
    slots = all_ref.shape[0]
    chunks = rows_here // SUB
    blocks = total // GROUP
    first = (lax.axis_index("rows") * n_cols + lax.axis_index("cols")) * rows_here

    def at(c):
        return pl.ds(pl.multiple_of(c * SUB, SUB), SUB)

    def loads(c):
        return (
            pltpu.make_async_copy(emb_ref.at[at(c), :], emb_buf.at[at(c), :], in_sem.at[0, c]),
            pltpu.make_async_copy(fac_ref.at[at(c), :], fac_buf.at[at(c), :], in_sem.at[1, c]),
        )

    def store(c):
        return pltpu.make_async_copy(new_buf.at[at(c), :], new_ref.at[at(c), :], out_sem.at[c])

    def start_loads(c, carry):
        for copy in loads(c):
            copy.start()
        return carry

    lax.fori_loop(0, chunks, start_loads, 0)

    sub = lax.broadcasted_iota(jnp.int32, (total, total), 0)
    lane = lax.broadcasted_iota(jnp.int32, (total, total), 1)
    eye = sub == lane
    ids = jnp.broadcast_to(piv_ref[...].astype(f32), (total, total))
    ids = jnp.sum(jnp.where(eye, ids, 0.0), axis=1, keepdims=True)
    place = lax.broadcasted_iota(jnp.int32, (total, slots), 0)
    slot = lax.broadcasted_iota(jnp.int32, (total, slots), 1)
    owner = lax.shift_right_logical(slot, PMAX.bit_length() - 1)
    low = (owner * rows_here).astype(f32)
    above = ids >= low
    before = total - jnp.sum(jnp.where(above, 1.0, 0.0), axis=0, keepdims=True)
    rank = place.astype(f32) - before
    chosen = above & (ids < low + rows_here) & (rank == (slot - owner * PMAX).astype(f32))
    chosen = jnp.where(chosen, 1.0, 0.0).astype(bf16)
    full_width = all_ref.shape[1]
    part = width // 2
    for start in range(0, full_width, part):
        size = min(part, full_width - start)
        piv_buf[:, start:start + size] = jnp.dot(
            chosen, all_ref[:, start:start + size], preferred_element_type=f32
        ).astype(bf16)
    emb = piv_buf[:, :width]
    fac = piv_buf[:, width:width + fac_width]
    count = piv_buf[:, width + fac_width:width + fac_width + 1].astype(f32)
    wide = emb.astype(f32)
    norm = lax.rsqrt(jnp.sum(wide * wide, axis=1, keepdims=True) / width + EPS)
    q = learn(count)

    def to_row(col):
        return jnp.sum(jnp.where(eye, col, 0.0), axis=0, keepdims=True)

    norm_row = to_row(norm) * (TAU * LOG2E / width)
    q_row = to_row(q)
    dots = lax.dot_general(emb, emb, NT, preferred_element_type=f32)
    shared = lax.dot_general(fac, fac, NT, preferred_element_type=f32)
    block = q * q_row * jnp.exp2(dots * norm * norm_row - TAU * LOG2E) - shared
    block = block + jnp.where(eye, RIDGE, 0.0)
    work[...] = block

    row8 = lax.broadcasted_iota(jnp.int32, (GROUP, total), 0)
    lane8 = lax.broadcasted_iota(jnp.int32, (GROUP, total), 1)

    def column(rows, j):
        col = jnp.sum(jnp.where(lane8 == j, rows, 0.0), axis=1, keepdims=True)
        return jnp.broadcast_to(col, (GROUP, total))

    def factor_step(b, carry):
        rows, left, before = carry
        start = pl.multiple_of(b * GROUP, GROUP)
        cols = [column(rows, start + i) for i in range(GROUP)]
        inside = (lane8 >= start) & (lane8 < start + GROUP)
        mine = jnp.where(inside, jnp.where(lane8 == start + row8, 1.0, 0.0), rows)
        delta = lax.dot_general(
            left, before, (((0,), (0,)), ((), ())),
            precision=lax.Precision.HIGHEST, preferred_element_type=f32,
        )
        keep = jnp.where((lane >= start - GROUP) & (lane < start), 0.0, work[...])
        work[...] = keep - delta
        work[pl.ds(pl.multiple_of(jnp.maximum(start - GROUP, 0), GROUP), GROUP), :] = before
        later = pl.multiple_of(jnp.minimum(start + GROUP, total - GROUP), GROUP)
        ahead = work[pl.ds(later, GROUP), :]
        acols = [column(ahead, start + i) for i in range(GROUP)]
        ahead = jnp.where(inside, 0.0, ahead)
        diag = jnp.ones((GROUP, total), f32)
        for i in range(GROUP):
            d = cols[i][i:i + 1, :]
            diag = jnp.where(row8 == i, d, diag)
            r = 1.0 / d
            m = jnp.where(row8 > i, cols[i] * r, 0.0)
            am = acols[i] * r
            for n in range(i + 1, GROUP):
                top = cols[n][i:i + 1, :]
                cols[n] = cols[n] - m * top
                acols[n] = acols[n] - am * top
            top = mine[i:i + 1, :]
            mine = mine - m * top
            ahead = ahead - am * top
        mine = mine * lax.rsqrt(diag)
        left = jnp.where(lane8 >= start + GROUP, mine, 0.0)
        return ahead, left, mine

    wide_sub = lax.broadcasted_iota(jnp.int32, (LANES, LANES), 0)
    wide_lane = lax.broadcasted_iota(jnp.int32, (LANES, LANES), 1)
    small_eye = wide_sub == wide_lane
    ones = jnp.ones((2 * LANES, LANES), bf16)
    row = lax.broadcasted_iota(jnp.int32, (SUB, total), 0)
    here = piv_ref[...] - first

    def lane_sum(x):
        x = x.astype(f32)
        x = x * x
        acc = x[:, :LANES]
        for k in range(LANES, x.shape[1], LANES):
            acc = acc + x[:, k:k + LANES]
        hi, lo = split(acc)
        return jnp.dot(jnp.concatenate([hi, lo], axis=1), ones, preferred_element_type=f32)

    def spread(x):
        return jnp.concatenate([x] * (total // LANES), axis=1)

    def lines(x):
        return [
            jnp.sum(jnp.where(small_eye, x[g:g + LANES, :], 0.0), axis=0, keepdims=True)
            for g in range(0, SUB, LANES)
        ]

    def panel_step(c):
        for copy in loads(c):
            copy.wait()
        emb = emb_buf[at(c), :]
        fac = fac_buf[at(c), :]
        dots = lax.dot_general(emb, piv_buf[:, :width], NT, preferred_element_type=f32)
        shared = lax.dot_general(
            fac, piv_buf[:, width:width + fac_width], NT, preferred_element_type=f32
        )
        norm = lax.rsqrt(lane_sum(emb) / width + EPS)
        used = lane_sum(fac)
        counts = [
            jnp.where(small_eye, solved_ref[pl.ds(c * (SUB // LANES) + g, 1), :].astype(f32), 0.0)
            for g in range(SUB // LANES)
        ]
        counts = jnp.concatenate(counts, axis=0).astype(bf16)
        q = learn(jnp.dot(counts, ones[:LANES, :], preferred_element_type=f32))
        panel = spread(q) * q_row * jnp.exp2(dots * spread(norm) * norm_row - TAU * LOG2E) - shared
        panel = jnp.where(row == here - c * SUB, panel + RIDGE, panel)
        hi, lo = split(panel)
        hi_buf[at(c), :] = hi
        lo_buf[at(c), :] = lo
        for g, line in enumerate(lines(q * q + RIDGE - used)):
            gain_ref[pl.ds(c * (SUB // LANES) + g, 1), :] = line

    def both(b, carry):
        carry = factor_step(b, carry)
        panel_step(b)
        return carry

    def panel_only(c, carry):
        panel_step(c)
        return carry

    shared_steps = min(blocks, chunks)
    zero = jnp.zeros((GROUP, total), f32)
    carry = lax.fori_loop(0, shared_steps, both, (block[:GROUP, :], zero, zero))
    carry = lax.fori_loop(shared_steps, blocks, factor_step, carry)
    lax.fori_loop(shared_steps, chunks, panel_only, 0)
    work[total - GROUP:, :] = carry[2]
    hi_w, lo_w = split(jnp.where(lane <= sub, work[...], 0.0))

    def solve_step(c, best):
        hi = hi_buf[at(c), :]
        lo = lo_buf[at(c), :]
        full = (
            lax.dot_general(hi, hi_w, NT, preferred_element_type=f32)
            + lax.dot_general(hi, lo_w, NT, preferred_element_type=f32)
            + lax.dot_general(lo, hi_w, NT, preferred_element_type=f32)
        )
        new_buf[at(c), :] = full.astype(bf16)
        store(c).start()
        for g, line in enumerate(lines(lane_sum(full))):
            where = pl.ds(c * (SUB // LANES) + g, 1)
            gain = gain_ref[where, :] - line
            gain_ref[where, :] = gain
            best = jnp.maximum(best, gain)
        return best

    best = lax.fori_loop(0, chunks, solve_step, jnp.full((1, LANES), -jnp.inf, f32))
    best_ref[...] = jnp.broadcast_to(best, best_ref.shape)

    def finish(c, carry):
        store(c).wait()
        return carry

    lax.fori_loop(0, chunks, finish, 0)


def best_kernel(n_rows, n_cols, own_ref, out_ref, stage, buf_r, buf_c, send_r, recv_r, send_c, recv_c):
    r = lax.axis_index("rows")
    c = lax.axis_index("cols")
    barrier = pltpu.get_barrier_semaphore()
    peers_r = [(lax.rem(r + j, n_rows), c) for j in range(1, n_rows)]
    peers_c = [(r, lax.rem(c + i, n_cols)) for i in range(1, n_cols)]
    for peer in peers_r + peers_c:
        pl.semaphore_signal(barrier, inc=1, device_id=peer, device_id_type=MESH)
    pl.semaphore_wait(barrier, len(peers_r) + len(peers_c))

    def exchange(src, buf, send_sem, recv_sem, peers):
        copies = []
        for j, peer in enumerate(peers):
            copy = pltpu.make_async_remote_copy(
                src_ref=src, dst_ref=buf.at[j], send_sem=send_sem.at[j],
                recv_sem=recv_sem.at[j], device_id=peer, device_id_type=MESH,
            )
            copy.start()
            copies.append(copy)
        top = src[...]
        for j, copy in enumerate(copies):
            copy.wait_recv()
            top = jnp.maximum(top, buf[j])
        for copy in copies:
            copy.wait_send()
        return top

    stage[...] = exchange(own_ref, buf_r, send_r, recv_r, peers_r)
    out_ref[0, 0] = jnp.max(exchange(stage, buf_c, send_c, recv_c, peers_c))


def body(n_rows, n_cols, embeddings, factor_cols, solved, pivots):
    rows_here, width = embeddings.shape
    fac_width = factor_cols.shape[1]
    total = pivots.shape[0]
    devices = n_rows * n_cols
    packet = width + fac_width + LANES
    bf16 = jnp.bfloat16
    vmem = pl.BlockSpec(memory_space=pltpu.VMEM)
    smem = pl.BlockSpec(memory_space=pltpu.SMEM)
    params = functools.partial(pltpu.CompilerParams, vmem_limit_bytes=VMEM_LIMIT)
    own = pl.pallas_call(
        functools.partial(pick_kernel, n_cols),
        out_shape=jax.ShapeDtypeStruct((PMAX, packet), bf16),
        in_specs=[smem, smem, pl.BlockSpec(memory_space=pl.ANY), pl.BlockSpec(memory_space=pl.ANY)],
        out_specs=vmem,
        scratch_shapes=[
            pltpu.VMEM((16 * PMAX, width), bf16),
            pltpu.VMEM((16 * PMAX, fac_width), bf16),
            pltpu.SemaphoreType.DMA((2, PMAX)),
        ],
        compiler_params=params(),
        name="pick",
    )(pivots, solved, embeddings, factor_cols)
    everyone = pl.pallas_call(
        functools.partial(gather_kernel, n_rows, n_cols),
        out_shape=jax.ShapeDtypeStruct((devices, PMAX, packet), bf16),
        in_specs=[vmem],
        out_specs=vmem,
        scratch_shapes=[
            pltpu.SemaphoreType.DMA((devices,)),
            pltpu.SemaphoreType.DMA((devices,)),
            pltpu.SemaphoreType.DMA,
        ],
        compiler_params=params(collective_id=0, has_side_effects=True),
        name="gather",
    )(own)
    lines = rows_here // LANES
    hbm = pl.BlockSpec(memory_space=pl.ANY)
    chunks = rows_here // SUB
    new_cols, gains, best = pl.pallas_call(
        functools.partial(main_kernel, n_cols),
        out_shape=[
            jax.ShapeDtypeStruct((rows_here, total), bf16),
            jax.ShapeDtypeStruct((lines, LANES), jnp.float32),
            jax.ShapeDtypeStruct((8, LANES), jnp.float32),
        ],
        in_specs=[vmem, vmem, vmem, hbm, hbm],
        out_specs=[hbm, vmem, vmem],
        scratch_shapes=[
            pltpu.VMEM((rows_here, width), bf16),
            pltpu.VMEM((rows_here, fac_width), bf16),
            pltpu.VMEM((rows_here, total), bf16),
            pltpu.VMEM((rows_here, total), bf16),
            pltpu.VMEM((rows_here, total), bf16),
            pltpu.VMEM((total, packet), bf16),
            pltpu.VMEM((total, total), jnp.float32),
            pltpu.SemaphoreType.DMA((2, chunks)),
            pltpu.SemaphoreType.DMA((chunks,)),
        ],
        compiler_params=params(),
        name="main",
    )(
        pivots.reshape(1, total), everyone.reshape(devices * PMAX, packet),
        solved.reshape(lines, LANES), embeddings, factor_cols,
    )
    top = pl.pallas_call(
        functools.partial(best_kernel, n_rows, n_cols),
        out_shape=jax.ShapeDtypeStruct((1, 1), jnp.float32),
        in_specs=[vmem],
        out_specs=smem,
        scratch_shapes=[
            pltpu.VMEM((8, LANES), jnp.float32),
            pltpu.VMEM((n_rows, 8, LANES), jnp.float32),
            pltpu.VMEM((n_cols, 8, LANES), jnp.float32),
            pltpu.SemaphoreType.DMA((n_rows,)),
            pltpu.SemaphoreType.DMA((n_rows,)),
            pltpu.SemaphoreType.DMA((n_cols,)),
            pltpu.SemaphoreType.DMA((n_cols,)),
        ],
        compiler_params=params(collective_id=1, has_side_effects=True),
        name="best",
    )(best)
    return new_cols, gains.reshape(rows_here), top.reshape(())


def solution(mesh):
    n_rows, n_cols = mesh.shape["rows"], mesh.shape["cols"]
    in_specs = (P(("rows", "cols"), None), P(("rows", "cols"), None), P(("rows", "cols")), P())
    out_specs = (P(("rows", "cols"), None), P(("rows", "cols")), P())
    return jax.shard_map(
        functools.partial(body, n_rows, n_cols),
        mesh=mesh, in_specs=in_specs, out_specs=out_specs, check_vma=False,
    )
```

```python
import functools

import jax
import jax.numpy as jnp
from jax import lax
from jax.experimental import pallas as pl
from jax.experimental.pallas import tpu as pltpu
from jax.sharding import PartitionSpec as P

PMAX = 16
EPS = 1e-06
TAU = 6.0
RIDGE = 1.0
LOG2E = 1.4426950408889634
LANES = 128
GROUP = 8
SUB = 256
VMEM_LIMIT = 56 * 1024 * 1024
MESH = pl.DeviceIdType.MESH
NT = (((1,), (1,)), ((), ()))


def learn(counts):
    c = counts.astype(jnp.float32)
    return (c * (16.0 - c) + 8.0) / 72.0


def pick_kernel(n_cols, piv_ref, solved_ref, emb_ref, fac_ref, out_ref, ebuf, fbuf, sem):
    rows_here, width = emb_ref.shape
    fac_width = fac_ref.shape[1]
    total = piv_ref.shape[0]
    first = (lax.axis_index("rows") * n_cols + lax.axis_index("cols")) * rows_here
    before = jnp.int32(0)
    step = 1
    while step * 2 <= total:
        step *= 2
    while step:
        probe = jnp.minimum(before + step - 1, total - 1)
        inside = before + step <= total
        before = before + jnp.where(inside & (piv_ref[probe] < first), step, 0)
        step //= 2
    copies = []
    spots = []
    for r in range(PMAX):
        idx = jnp.clip(piv_ref[jnp.minimum(before + r, total - 1)] - first, 0, rows_here - 1)
        base = pl.multiple_of(lax.shift_left(lax.shift_right_logical(idx, 4), 4), 16)
        for src, dst, k in ((emb_ref, ebuf, 0), (fac_ref, fbuf, 1)):
            copy = pltpu.make_async_copy(
                src.at[pl.ds(base, 16), :], dst.at[pl.ds(16 * r, 16), :], sem.at[k, r]
            )
            copy.start()
            copies.append(copy)
        spots.append((idx, idx - base + 16 * r))
    row = lax.broadcasted_iota(jnp.int32, (PMAX, 16 * PMAX), 0)
    lane = lax.broadcasted_iota(jnp.int32, (PMAX, 16 * PMAX), 1)
    row1 = lax.broadcasted_iota(jnp.int32, (PMAX, LANES), 0)
    want = jnp.zeros((PMAX, 16 * PMAX), jnp.int32)
    count = jnp.zeros((PMAX, LANES), jnp.int32)
    for r, (idx, spot) in enumerate(spots):
        want = jnp.where(row == r, spot, want)
        count = jnp.where(row1 == r, solved_ref[idx], count)
    pick = jnp.where(lane == want, 1.0, 0.0).astype(jnp.bfloat16)
    out_ref[:, width + fac_width:] = count.astype(jnp.float32).astype(jnp.bfloat16)
    for copy in copies:
        copy.wait()
    out_ref[:, :width] = jnp.dot(
        pick, ebuf[...], preferred_element_type=jnp.float32
    ).astype(jnp.bfloat16)
    out_ref[:, width:width + fac_width] = jnp.dot(
        pick, fbuf[...], preferred_element_type=jnp.float32
    ).astype(jnp.bfloat16)


def gather_kernel(n_rows, n_cols, own_ref, out_ref, send_sem, recv_sem, own_sem):
    r = lax.axis_index("rows")
    c = lax.axis_index("cols")
    pairs = n_cols // 2
    h = c // 2
    k = c - 2 * h
    twin = 2 * h + 1 - k

    def other_row(j):
        return lax.rem(r + j, n_rows)

    def other_col(i):
        return 2 * lax.rem(h + i, pairs) + k

    barrier = pltpu.get_barrier_semaphore()
    peers = [(other_row(j), c) for j in range(1, n_rows)]
    peers += [(r, other_col(i)) for i in range(1, pairs)]
    peers.append((r, twin))
    for peer in peers:
        pl.semaphore_signal(barrier, inc=1, device_id=peer, device_id_type=MESH)
    own = pltpu.make_async_copy(own_ref, out_ref.at[r * n_cols + c], own_sem)
    own.start()
    pl.semaphore_wait(barrier, len(peers))

    sent = []

    def send(src, block, peer):
        copy = pltpu.make_async_remote_copy(
            src_ref=src,
            dst_ref=out_ref.at[block],
            send_sem=send_sem.at[len(sent)],
            recv_sem=recv_sem.at[block],
            device_id=peer,
            device_id_type=MESH,
        )
        copy.start()
        sent.append(copy)

    def arrived(block):
        pltpu.make_async_remote_copy(
            src_ref=own_ref,
            dst_ref=out_ref.at[block],
            send_sem=send_sem.at[0],
            recv_sem=recv_sem.at[block],
            device_id=(r, twin),
            device_id_type=MESH,
        ).wait_recv()

    me = r * n_cols + c
    for i in range(1, pairs):
        send(own_ref, me, (r, other_col(i)))
    for j in range(1, n_rows):
        send(own_ref, me, (other_row(j), c))
    send(own_ref, me, (r, twin))
    order = [j for j in range(1, n_rows)]
    for j in order:
        block = other_row(j) * n_cols + c
        arrived(block)
        for i in range(1, pairs):
            send(out_ref.at[block], block, (r, other_col(i)))
        send(out_ref.at[block], block, (r, twin))
    for j in [0] + order:
        for i in range(1, pairs):
            block = other_row(j) * n_cols + other_col(i)
            arrived(block)
            send(out_ref.at[block], block, (r, twin))
    for j in range(n_rows):
        for i in range(pairs):
            arrived(other_row(j) * n_cols + 2 * lax.rem(h + i, pairs) + 1 - k)
    own.wait()
    for copy in sent:
        copy.wait_send()


def split(x):
    hi = x.astype(jnp.bfloat16)
    return hi, (x - hi.astype(jnp.float32)).astype(jnp.bfloat16)


def main_kernel(
    n_cols, piv_ref, all_ref, solved_ref, emb_ref, fac_ref,
    new_ref, gain_ref, best_ref,
    emb_buf, fac_buf, hi_buf, lo_buf, new_buf, piv_buf, turn_buf, work, in_sem, out_sem,
):
    f32, bf16 = jnp.float32, jnp.bfloat16
    rows_here, width = emb_ref.shape
    fac_width = fac_ref.shape[1]
    total = piv_ref.shape[1]
    slots = all_ref.shape[0]
    chunks = rows_here // SUB
    blocks = total // GROUP
    first = (lax.axis_index("rows") * n_cols + lax.axis_index("cols")) * rows_here

    def at(c):
        return pl.ds(pl.multiple_of(c * SUB, SUB), SUB)

    def loads(c):
        return (
            pltpu.make_async_copy(emb_ref.at[at(c), :], emb_buf.at[at(c), :], in_sem.at[0, c]),
            pltpu.make_async_copy(fac_ref.at[at(c), :], fac_buf.at[at(c), :], in_sem.at[1, c]),
        )

    def store(c):
        return pltpu.make_async_copy(new_buf.at[at(c), :], new_ref.at[at(c), :], out_sem.at[c])

    def start_loads(c, carry):
        for copy in loads(c):
            copy.start()
        return carry

    lax.fori_loop(0, chunks, start_loads, 0)

    sub = lax.broadcasted_iota(jnp.int32, (total, total), 0)
    lane = lax.broadcasted_iota(jnp.int32, (total, total), 1)
    eye = sub == lane
    ids = jnp.broadcast_to(piv_ref[...].astype(f32), (total, total))
    ids = jnp.sum(jnp.where(eye, ids, 0.0), axis=1, keepdims=True)
    place = lax.broadcasted_iota(jnp.int32, (total, slots), 0)
    slot = lax.broadcasted_iota(jnp.int32, (total, slots), 1)
    owner = lax.shift_right_logical(slot, PMAX.bit_length() - 1)
    low = (owner * rows_here).astype(f32)
    above = ids >= low
    before = total - jnp.sum(jnp.where(above, 1.0, 0.0), axis=0, keepdims=True)
    rank = place.astype(f32) - before
    chosen = above & (ids < low + rows_here) & (rank == (slot - owner * PMAX).astype(f32))
    chosen = jnp.where(chosen, 1.0, 0.0).astype(bf16)
    full_width = all_ref.shape[1]
    part = width // 2
    for start in range(0, full_width, part):
        size = min(part, full_width - start)
        piv_buf[:, start:start + size] = jnp.dot(
            chosen, all_ref[:, start:start + size], preferred_element_type=f32
        ).astype(bf16)
    emb = piv_buf[:, :width]
    fac = piv_buf[:, width:width + fac_width]
    count = piv_buf[:, width + fac_width:width + fac_width + 1].astype(f32)
    wide = emb.astype(f32)
    norm = lax.rsqrt(jnp.sum(wide * wide, axis=1, keepdims=True) / width + EPS)
    q = learn(count)

    def to_row(col):
        return jnp.sum(jnp.where(eye, col, 0.0), axis=0, keepdims=True)

    norm_row = to_row(norm) * (TAU * LOG2E / width)
    q_row = to_row(q)
    used_width = width + fac_width
    for start in range(0, used_width, LANES):
        turn_buf[start:start + LANES, :] = (
            piv_buf[:, start:start + LANES].astype(f32).T.astype(bf16)
        )
    dots = jnp.dot(emb, turn_buf[:width, :], preferred_element_type=f32)
    shared = jnp.dot(fac, turn_buf[width:, :], preferred_element_type=f32)
    block = q * q_row * jnp.exp2(dots * norm * norm_row - TAU * LOG2E) - shared
    block = block + jnp.where(eye, RIDGE, 0.0)
    work[...] = block

    row8 = lax.broadcasted_iota(jnp.int32, (GROUP, total), 0)
    lane8 = lax.broadcasted_iota(jnp.int32, (GROUP, total), 1)

    def column(rows, j):
        col = jnp.sum(jnp.where(lane8 == j, rows, 0.0), axis=1, keepdims=True)
        return jnp.broadcast_to(col, (GROUP, total))

    def factor_step(b, carry):
        rows, left, before = carry
        start = pl.multiple_of(b * GROUP, GROUP)
        cols = [column(rows, start + i) for i in range(GROUP)]
        inside = (lane8 >= start) & (lane8 < start + GROUP)
        mine = jnp.where(inside, jnp.where(lane8 == start + row8, 1.0, 0.0), rows)
        delta = lax.dot_general(
            left, before, (((0,), (0,)), ((), ())),
            precision=lax.Precision.HIGHEST, preferred_element_type=f32,
        )
        keep = jnp.where((lane >= start - GROUP) & (lane < start), 0.0, work[...])
        work[...] = keep - delta
        work[pl.ds(pl.multiple_of(jnp.maximum(start - GROUP, 0), GROUP), GROUP), :] = before
        later = pl.multiple_of(jnp.minimum(start + GROUP, total - GROUP), GROUP)
        ahead = work[pl.ds(later, GROUP), :]
        acols = [column(ahead, start + i) for i in range(GROUP)]
        ahead = jnp.where(inside, 0.0, ahead)
        diag = jnp.ones((GROUP, total), f32)
        for i in range(GROUP):
            d = cols[i][i:i + 1, :]
            diag = jnp.where(row8 == i, d, diag)
            r = 1.0 / d
            m = jnp.where(row8 > i, cols[i] * r, 0.0)
            am = acols[i] * r
            for n in range(i + 1, GROUP):
                top = cols[n][i:i + 1, :]
                cols[n] = cols[n] - m * top
                acols[n] = acols[n] - am * top
            top = mine[i:i + 1, :]
            mine = mine - m * top
            ahead = ahead - am * top
        mine = mine * lax.rsqrt(diag)
        left = jnp.where(lane8 >= start + GROUP, mine, 0.0)
        return ahead, left, mine

    wide_sub = lax.broadcasted_iota(jnp.int32, (LANES, LANES), 0)
    wide_lane = lax.broadcasted_iota(jnp.int32, (LANES, LANES), 1)
    small_eye = wide_sub == wide_lane
    ones = jnp.ones((2 * LANES, LANES), bf16)
    row = lax.broadcasted_iota(jnp.int32, (SUB, total), 0)
    here = piv_ref[...] - first

    def lane_sum(x):
        x = x.astype(f32)
        x = x * x
        acc = x[:, :LANES]
        for k in range(LANES, x.shape[1], LANES):
            acc = acc + x[:, k:k + LANES]
        hi, lo = split(acc)
        return jnp.dot(jnp.concatenate([hi, lo], axis=1), ones, preferred_element_type=f32)

    def spread(x):
        return jnp.concatenate([x] * (total // LANES), axis=1)

    def lines(x):
        return [
            jnp.sum(jnp.where(small_eye, x[g:g + LANES, :], 0.0), axis=0, keepdims=True)
            for g in range(0, SUB, LANES)
        ]

    def panel_step(c):
        for copy in loads(c):
            copy.wait()
        emb = emb_buf[at(c), :]
        fac = fac_buf[at(c), :]
        dots = jnp.dot(emb, turn_buf[:width, :], preferred_element_type=f32)
        shared = jnp.dot(fac, turn_buf[width:, :], preferred_element_type=f32)
        norm = lax.rsqrt(lane_sum(emb) / width + EPS)
        used = lane_sum(fac)
        counts = [
            jnp.where(small_eye, solved_ref[pl.ds(c * (SUB // LANES) + g, 1), :].astype(f32), 0.0)
            for g in range(SUB // LANES)
        ]
        counts = jnp.concatenate(counts, axis=0).astype(bf16)
        q = learn(jnp.dot(counts, ones[:LANES, :], preferred_element_type=f32))
        panel = spread(q) * q_row * jnp.exp2(dots * spread(norm) * norm_row - TAU * LOG2E) - shared
        panel = jnp.where(row == here - c * SUB, panel + RIDGE, panel)
        hi, lo = split(panel)
        hi_buf[at(c), :] = hi
        lo_buf[at(c), :] = lo
        for g, line in enumerate(lines(q * q + RIDGE - used)):
            gain_ref[pl.ds(c * (SUB // LANES) + g, 1), :] = line

    def both(b, carry):
        carry = factor_step(b, carry)
        panel_step(b)
        return carry

    def panel_only(c, carry):
        panel_step(c)
        return carry

    shared_steps = min(blocks, chunks)
    zero = jnp.zeros((GROUP, total), f32)
    carry = lax.fori_loop(0, shared_steps, both, (block[:GROUP, :], zero, zero))
    carry = lax.fori_loop(shared_steps, blocks, factor_step, carry)
    lax.fori_loop(shared_steps, chunks, panel_only, 0)
    work[total - GROUP:, :] = carry[2]
    hi_w, lo_w = split(jnp.where(lane <= sub, work[...], 0.0).T)
    triple = jnp.concatenate([hi_w, lo_w, hi_w], axis=0)

    def solve_step(c, best):
        hi = hi_buf[at(c), :]
        lo = lo_buf[at(c), :]
        full = jnp.dot(
            jnp.concatenate([hi, hi, lo], axis=1), triple, preferred_element_type=f32
        )
        new_buf[at(c), :] = full.astype(bf16)
        store(c).start()
        for g, line in enumerate(lines(lane_sum(full))):
            where = pl.ds(c * (SUB // LANES) + g, 1)
            gain = gain_ref[where, :] - line
            gain_ref[where, :] = gain
            best = jnp.maximum(best, gain)
        return best

    best = lax.fori_loop(0, chunks, solve_step, jnp.full((1, LANES), -jnp.inf, f32))
    best_ref[...] = jnp.broadcast_to(best, best_ref.shape)

    def finish(c, carry):
        store(c).wait()
        return carry

    lax.fori_loop(0, chunks, finish, 0)


def best_kernel(n_rows, n_cols, own_ref, out_ref, buf, send_sem, recv_sem):
    r = lax.axis_index("rows")
    c = lax.axis_index("cols")
    peers = [
        (lax.rem(r + j, n_rows), lax.rem(c + i, n_cols))
        for j in range(n_rows) for i in range(n_cols) if i or j
    ]
    barrier = pltpu.get_barrier_semaphore()
    for peer in peers:
        pl.semaphore_signal(barrier, inc=1, device_id=peer, device_id_type=MESH)
    pl.semaphore_wait(barrier, len(peers))
    copies = []
    for j, peer in enumerate(peers):
        copy = pltpu.make_async_remote_copy(
            src_ref=own_ref, dst_ref=buf.at[j], send_sem=send_sem.at[j],
            recv_sem=recv_sem.at[j], device_id=peer, device_id_type=MESH,
        )
        copy.start()
        copies.append(copy)
    top = own_ref[...]
    for j, copy in enumerate(copies):
        copy.wait_recv()
        top = jnp.maximum(top, buf[j])
    out_ref[0, 0] = jnp.max(top)
    for copy in copies:
        copy.wait_send()


def body(n_rows, n_cols, embeddings, factor_cols, solved, pivots):
    rows_here, width = embeddings.shape
    fac_width = factor_cols.shape[1]
    total = pivots.shape[0]
    devices = n_rows * n_cols
    packet = width + fac_width + LANES
    bf16 = jnp.bfloat16
    vmem = pl.BlockSpec(memory_space=pltpu.VMEM)
    smem = pl.BlockSpec(memory_space=pltpu.SMEM)
    params = functools.partial(pltpu.CompilerParams, vmem_limit_bytes=VMEM_LIMIT)
    own = pl.pallas_call(
        functools.partial(pick_kernel, n_cols),
        out_shape=jax.ShapeDtypeStruct((PMAX, packet), bf16),
        in_specs=[smem, smem, pl.BlockSpec(memory_space=pl.ANY), pl.BlockSpec(memory_space=pl.ANY)],
        out_specs=vmem,
        scratch_shapes=[
            pltpu.VMEM((16 * PMAX, width), bf16),
            pltpu.VMEM((16 * PMAX, fac_width), bf16),
            pltpu.SemaphoreType.DMA((2, PMAX)),
        ],
        compiler_params=params(),
        name="pick",
    )(pivots, solved, embeddings, factor_cols)
    everyone = pl.pallas_call(
        functools.partial(gather_kernel, n_rows, n_cols),
        out_shape=jax.ShapeDtypeStruct((devices, PMAX, packet), bf16),
        in_specs=[vmem],
        out_specs=vmem,
        scratch_shapes=[
            pltpu.SemaphoreType.DMA((devices,)),
            pltpu.SemaphoreType.DMA((devices,)),
            pltpu.SemaphoreType.DMA,
        ],
        compiler_params=params(collective_id=0, has_side_effects=True),
        name="gather",
    )(own)
    lines = rows_here // LANES
    hbm = pl.BlockSpec(memory_space=pl.ANY)
    chunks = rows_here // SUB
    new_cols, gains, best = pl.pallas_call(
        functools.partial(main_kernel, n_cols),
        out_shape=[
            jax.ShapeDtypeStruct((rows_here, total), bf16),
            jax.ShapeDtypeStruct((lines, LANES), jnp.float32),
            jax.ShapeDtypeStruct((8, LANES), jnp.float32),
        ],
        in_specs=[vmem, vmem, vmem, hbm, hbm],
        out_specs=[hbm, vmem, vmem],
        scratch_shapes=[
            pltpu.VMEM((rows_here, width), bf16),
            pltpu.VMEM((rows_here, fac_width), bf16),
            pltpu.VMEM((rows_here, total), bf16),
            pltpu.VMEM((rows_here, total), bf16),
            pltpu.VMEM((rows_here, total), bf16),
            pltpu.VMEM((total, packet), bf16),
            pltpu.VMEM((width + fac_width, total), bf16),
            pltpu.VMEM((total, total), jnp.float32),
            pltpu.SemaphoreType.DMA((2, chunks)),
            pltpu.SemaphoreType.DMA((chunks,)),
        ],
        compiler_params=params(),
        name="main",
    )(
        pivots.reshape(1, total), everyone.reshape(devices * PMAX, packet),
        solved.reshape(lines, LANES), embeddings, factor_cols,
    )
    top = pl.pallas_call(
        functools.partial(best_kernel, n_rows, n_cols),
        out_shape=jax.ShapeDtypeStruct((1, 1), jnp.float32),
        in_specs=[vmem],
        out_specs=smem,
        scratch_shapes=[
            pltpu.VMEM((devices - 1, 8, LANES), jnp.float32),
            pltpu.SemaphoreType.DMA((devices - 1,)),
            pltpu.SemaphoreType.DMA((devices - 1,)),
        ],
        compiler_params=params(collective_id=1, has_side_effects=True),
        name="best",
    )(best)
    return new_cols, gains.reshape(rows_here), top.reshape(())


def solution(mesh):
    n_rows, n_cols = mesh.shape["rows"], mesh.shape["cols"]
    in_specs = (P(("rows", "cols"), None), P(("rows", "cols"), None), P(("rows", "cols")), P())
    out_specs = (P(("rows", "cols"), None), P(("rows", "cols")), P())
    return jax.shard_map(
        functools.partial(body, n_rows, n_cols),
        mesh=mesh, in_specs=in_specs, out_specs=out_specs, check_vma=False,
    )
```

```python
import functools

import jax
import jax.numpy as jnp
from jax import lax
from jax.experimental import pallas as pl
from jax.experimental.pallas import tpu as pltpu
from jax.sharding import PartitionSpec as P

PMAX = 16
EPS = 1e-06
TAU = 6.0
RIDGE = 1.0
LOG2E = 1.4426950408889634
LANES = 128
GROUP = 8
SUB = 256
PIECE = 32
VMEM_LIMIT = 56 * 1024 * 1024
MESH = pl.DeviceIdType.MESH
NT = (((1,), (1,)), ((), ()))


def learn(counts):
    c = counts.astype(jnp.float32)
    return (c * (16.0 - c) + 8.0) / 72.0


def pick_kernel(n_cols, piv_ref, solved_ref, emb_ref, fac_ref, out_ref, ebuf, fbuf, sem):
    rows_here, width = emb_ref.shape
    fac_width = fac_ref.shape[1]
    total = piv_ref.shape[0]
    first = (lax.axis_index("rows") * n_cols + lax.axis_index("cols")) * rows_here
    before = jnp.int32(0)
    step = 1
    while step * 2 <= total:
        step *= 2
    while step:
        probe = jnp.minimum(before + step - 1, total - 1)
        inside = before + step <= total
        before = before + jnp.where(inside & (piv_ref[probe] < first), step, 0)
        step //= 2
    copies = []
    spots = []
    for r in range(PMAX):
        idx = jnp.clip(piv_ref[jnp.minimum(before + r, total - 1)] - first, 0, rows_here - 1)
        base = pl.multiple_of(lax.shift_left(lax.shift_right_logical(idx, 4), 4), 16)
        for src, dst, k in ((emb_ref, ebuf, 0), (fac_ref, fbuf, 1)):
            copy = pltpu.make_async_copy(
                src.at[pl.ds(base, 16), :], dst.at[pl.ds(16 * r, 16), :], sem.at[k, r]
            )
            copy.start()
            copies.append(copy)
        spots.append((idx, idx - base + 16 * r))
    row = lax.broadcasted_iota(jnp.int32, (PMAX, 16 * PMAX), 0)
    lane = lax.broadcasted_iota(jnp.int32, (PMAX, 16 * PMAX), 1)
    row1 = lax.broadcasted_iota(jnp.int32, (PMAX, LANES), 0)
    want = jnp.zeros((PMAX, 16 * PMAX), jnp.int32)
    count = jnp.zeros((PMAX, LANES), jnp.int32)
    for r, (idx, spot) in enumerate(spots):
        want = jnp.where(row == r, spot, want)
        count = jnp.where(row1 == r, solved_ref[idx], count)
    pick = jnp.where(lane == want, 1.0, 0.0).astype(jnp.bfloat16)
    out_ref[:, width + fac_width:] = count.astype(jnp.float32).astype(jnp.bfloat16)
    for copy in copies:
        copy.wait()
    out_ref[:, :width] = jnp.dot(
        pick, ebuf[...], preferred_element_type=jnp.float32
    ).astype(jnp.bfloat16)
    out_ref[:, width:width + fac_width] = jnp.dot(
        pick, fbuf[...], preferred_element_type=jnp.float32
    ).astype(jnp.bfloat16)


def gather_kernel(n_rows, n_cols, own_ref, out_ref, send_sem, recv_sem, own_sem):
    r = lax.axis_index("rows")
    c = lax.axis_index("cols")
    pairs = n_cols // 2
    h = c // 2
    k = c - 2 * h
    twin = 2 * h + 1 - k

    def other_row(j):
        return lax.rem(r + j, n_rows)

    def other_col(i):
        return 2 * lax.rem(h + i, pairs) + k

    barrier = pltpu.get_barrier_semaphore()
    peers = [(other_row(j), c) for j in range(1, n_rows)]
    peers += [(r, other_col(i)) for i in range(1, pairs)]
    peers.append((r, twin))
    for peer in peers:
        pl.semaphore_signal(barrier, inc=1, device_id=peer, device_id_type=MESH)
    own = pltpu.make_async_copy(own_ref, out_ref.at[r * n_cols + c], own_sem)
    own.start()
    pl.semaphore_wait(barrier, len(peers))

    sent = []

    def send(src, block, peer):
        copy = pltpu.make_async_remote_copy(
            src_ref=src,
            dst_ref=out_ref.at[block],
            send_sem=send_sem.at[len(sent)],
            recv_sem=recv_sem.at[block],
            device_id=peer,
            device_id_type=MESH,
        )
        copy.start()
        sent.append(copy)

    def arrived(block):
        pltpu.make_async_remote_copy(
            src_ref=own_ref,
            dst_ref=out_ref.at[block],
            send_sem=send_sem.at[0],
            recv_sem=recv_sem.at[block],
            device_id=(r, twin),
            device_id_type=MESH,
        ).wait_recv()

    me = r * n_cols + c
    for i in range(1, pairs):
        send(own_ref, me, (r, other_col(i)))
    for j in range(1, n_rows):
        send(own_ref, me, (other_row(j), c))
    send(own_ref, me, (r, twin))
    order = [j for j in range(1, n_rows)]
    for j in order:
        block = other_row(j) * n_cols + c
        arrived(block)
        for i in range(1, pairs):
            send(out_ref.at[block], block, (r, other_col(i)))
        send(out_ref.at[block], block, (r, twin))
    for j in [0] + order:
        for i in range(1, pairs):
            block = other_row(j) * n_cols + other_col(i)
            arrived(block)
            send(out_ref.at[block], block, (r, twin))
    for j in range(n_rows):
        for i in range(pairs):
            arrived(other_row(j) * n_cols + 2 * lax.rem(h + i, pairs) + 1 - k)
    own.wait()
    for copy in sent:
        copy.wait_send()


def split(x):
    hi = x.astype(jnp.bfloat16)
    return hi, (x - hi.astype(jnp.float32)).astype(jnp.bfloat16)


def main_kernel(
    n_cols, piv_ref, all_ref, solved_ref, emb_ref, fac_ref,
    new_ref, gain_ref, best_ref,
    emb_buf, fac_buf, hi_buf, lo_buf, new_buf, piv_buf, turn_buf, work, delta_buf, dots_buf, shared_buf, stat_buf, sum_buf,
    in_sem, out_sem,
):
    f32, bf16 = jnp.float32, jnp.bfloat16
    rows_here, width = emb_ref.shape
    fac_width = fac_ref.shape[1]
    total = piv_ref.shape[1]
    slots = all_ref.shape[0]
    chunks = rows_here // SUB
    blocks = total // GROUP
    first = (lax.axis_index("rows") * n_cols + lax.axis_index("cols")) * rows_here

    def at(c):
        return pl.ds(pl.multiple_of(c * SUB, SUB), SUB)

    def loads(c):
        return (
            pltpu.make_async_copy(emb_ref.at[at(c), :], emb_buf.at[at(c), :], in_sem.at[0, c]),
            pltpu.make_async_copy(fac_ref.at[at(c), :], fac_buf.at[at(c), :], in_sem.at[1, c]),
        )

    def store(c):
        return pltpu.make_async_copy(new_buf.at[at(c), :], new_ref.at[at(c), :], out_sem.at[c])

    def start_loads(c, carry):
        for copy in loads(c):
            copy.start()
        return carry

    lax.fori_loop(0, chunks, start_loads, 0)

    sub = lax.broadcasted_iota(jnp.int32, (total, total), 0)
    lane = lax.broadcasted_iota(jnp.int32, (total, total), 1)
    eye = sub == lane
    ids = jnp.broadcast_to(piv_ref[...].astype(f32), (total, total))
    ids = jnp.sum(jnp.where(eye, ids, 0.0), axis=1, keepdims=True)
    place = lax.broadcasted_iota(jnp.int32, (total, slots), 0)
    slot = lax.broadcasted_iota(jnp.int32, (total, slots), 1)
    owner = lax.shift_right_logical(slot, PMAX.bit_length() - 1)
    low = (owner * rows_here).astype(f32)
    above = ids >= low
    before = total - jnp.sum(jnp.where(above, 1.0, 0.0), axis=0, keepdims=True)
    rank = place.astype(f32) - before
    chosen = above & (ids < low + rows_here) & (rank == (slot - owner * PMAX).astype(f32))
    chosen = jnp.where(chosen, 1.0, 0.0).astype(bf16)
    full_width = all_ref.shape[1]
    part = width // 2
    for start in range(0, full_width, part):
        size = min(part, full_width - start)
        piv_buf[:, start:start + size] = jnp.dot(
            chosen, all_ref[:, start:start + size], preferred_element_type=f32
        ).astype(bf16)
    emb = piv_buf[:, :width]
    fac = piv_buf[:, width:width + fac_width]
    count = piv_buf[:, width + fac_width:width + fac_width + 1].astype(f32)
    wide = emb.astype(f32)
    norm = lax.rsqrt(jnp.sum(wide * wide, axis=1, keepdims=True) / width + EPS)
    q = learn(count)

    def to_row(col):
        return jnp.sum(jnp.where(eye, col, 0.0), axis=0, keepdims=True)

    norm_row = to_row(norm) * (TAU * LOG2E / width)
    q_row = to_row(q)
    used_width = width + fac_width
    for start in range(0, used_width, LANES):
        turn_buf[start:start + LANES, :] = (
            piv_buf[:, start:start + LANES].astype(f32).T.astype(bf16)
        )
    dots = jnp.dot(emb, turn_buf[:width, :], preferred_element_type=f32)
    shared = jnp.dot(fac, turn_buf[width:, :], preferred_element_type=f32)
    block = q * q_row * jnp.exp2(dots * norm * norm_row - TAU * LOG2E) - shared
    block = block + jnp.where(eye, RIDGE, 0.0)
    work[...] = block

    row8 = lax.broadcasted_iota(jnp.int32, (GROUP, total), 0)
    lane8 = lax.broadcasted_iota(jnp.int32, (GROUP, total), 1)

    lane_piece = lax.broadcasted_iota(jnp.int32, (PIECE, total), 1)
    row_piece = lax.broadcasted_iota(jnp.int32, (PIECE, total), 0)

    def column(rows, j):
        col = jnp.sum(jnp.where(lane8 == j, rows, 0.0), axis=1, keepdims=True)
        return jnp.broadcast_to(col, (GROUP, total))

    def factor_step(b, carry):
        rows, left, before = carry
        start = pl.multiple_of(b * GROUP, GROUP)
        cols = [column(rows, start + i) for i in range(GROUP)]
        inside = (lane8 >= start) & (lane8 < start + GROUP)
        mine = jnp.where(inside, jnp.where(lane8 == start + row8, 1.0, 0.0), rows)
        delta = lax.dot_general(
            left, before, (((0,), (0,)), ((), ())),
            precision=lax.Precision.HIGHEST, preferred_element_type=f32,
        )
        delta_buf[...] = delta
        gone = (lane_piece >= start - GROUP) & (lane_piece < start)
        for p in range(0, total, PIECE):
            work[p:p + PIECE, :] = (
                jnp.where(gone, 0.0, work[p:p + PIECE, :]) - delta_buf[p:p + PIECE, :]
            )
        work[pl.ds(pl.multiple_of(jnp.maximum(start - GROUP, 0), GROUP), GROUP), :] = before
        later = pl.multiple_of(jnp.minimum(start + GROUP, total - GROUP), GROUP)
        ahead = work[pl.ds(later, GROUP), :]
        acols = [column(ahead, start + i) for i in range(GROUP)]
        ahead = jnp.where(inside, 0.0, ahead)
        diag = jnp.ones((GROUP, total), f32)
        for i in range(GROUP):
            d = cols[i][i:i + 1, :]
            diag = jnp.where(row8 == i, d, diag)
            r = 1.0 / d
            m = jnp.where(row8 > i, cols[i] * r, 0.0)
            am = acols[i] * r
            for n in range(i + 1, GROUP):
                top = cols[n][i:i + 1, :]
                cols[n] = cols[n] - m * top
                acols[n] = acols[n] - am * top
            top = mine[i:i + 1, :]
            mine = mine - m * top
            ahead = ahead - am * top
        mine = mine * lax.rsqrt(diag)
        left = jnp.where(lane8 >= start + GROUP, mine, 0.0)
        return ahead, left, mine

    wide_sub = lax.broadcasted_iota(jnp.int32, (LANES, LANES), 0)
    wide_lane = lax.broadcasted_iota(jnp.int32, (LANES, LANES), 1)
    small_eye = wide_sub == wide_lane
    ones = jnp.ones((2 * LANES, LANES), bf16)
    eye_row = lax.broadcasted_iota(jnp.int32, (PIECE, LANES), 0)
    eye_lane = lax.broadcasted_iota(jnp.int32, (PIECE, LANES), 1)
    here = piv_ref[...] - first

    def squares(load, width, p, k):
        acc = jnp.zeros((PIECE, LANES), f32)
        for j in range(0, width, LANES):
            x = load(j).astype(f32)
            acc = acc + x * x
        hi, lo = split(acc)
        stat_buf[p:p + PIECE, k:k + LANES] = hi
        stat_buf[p:p + PIECE, k + LANES:k + 2 * LANES] = lo

    def row_sums(rows, k):
        return jnp.dot(stat_buf[:rows, k:k + 2 * LANES], ones, preferred_element_type=f32)

    def line_part(x, p):
        mine = eye_lane == eye_row + p % LANES
        return jnp.sum(jnp.where(mine, x, 0.0), axis=0, keepdims=True)

    def panel_step(c):
        base = pl.multiple_of(c * SUB, SUB)
        for copy in loads(c):
            copy.wait()
        dots_buf[...] = jnp.dot(
            emb_buf[at(c), :], turn_buf[:width, :], preferred_element_type=f32
        )
        shared_buf[...] = jnp.dot(
            fac_buf[at(c), :], turn_buf[width:, :], preferred_element_type=f32
        )
        for p in range(0, SUB, PIECE):
            rows = pl.ds(base + p, PIECE)
            squares(lambda j: emb_buf[rows, j:j + LANES], width, p, 0)
            squares(lambda j: fac_buf[rows, j:j + LANES], fac_width, p, 2 * LANES)
        sum_buf[:SUB, :LANES] = row_sums(SUB, 0)
        sum_buf[:SUB, LANES:2 * LANES] = row_sums(SUB, 2 * LANES)
        for g in range(SUB // LANES):
            line = solved_ref[pl.ds(c * (SUB // LANES) + g, 1), :].astype(f32)
            counts = jnp.where(small_eye, line, 0.0).astype(bf16)
            sum_buf[g * LANES:(g + 1) * LANES, 2 * LANES:] = jnp.dot(
                counts, ones[:LANES, :], preferred_element_type=f32
            )
        for g in range(SUB // LANES):
            line = jnp.zeros((1, LANES), f32)
            for p in range(g * LANES, (g + 1) * LANES, PIECE):
                rows = pl.ds(base + p, PIECE)
                norm = lax.rsqrt(sum_buf[p:p + PIECE, :LANES] / width + EPS)
                q = learn(sum_buf[p:p + PIECE, 2 * LANES:])
                line = line + line_part(
                    q * q + RIDGE - sum_buf[p:p + PIECE, LANES:2 * LANES], p
                )
                for k in range(0, total, LANES):
                    half = slice(k, k + LANES)
                    power = dots_buf[p:p + PIECE, half] * norm * norm_row[:, half] - TAU * LOG2E
                    panel = q * q_row[:, half] * jnp.exp2(power) - shared_buf[p:p + PIECE, half]
                    panel = jnp.where(
                        row_piece[:, half] == here[:, half] - (base + p), panel + RIDGE, panel
                    )
                    hi, lo = split(panel)
                    hi_buf[rows, half] = hi
                    lo_buf[rows, half] = lo
            gain_ref[pl.ds(c * (SUB // LANES) + g, 1), :] = line

    def both(b, carry):
        carry = factor_step(b, carry)
        panel_step(b)
        return carry

    def panel_only(c, carry):
        panel_step(c)
        return carry

    shared_steps = min(blocks, chunks)
    zero = jnp.zeros((GROUP, total), f32)
    carry = lax.fori_loop(0, shared_steps, both, (block[:GROUP, :], zero, zero))
    carry = lax.fori_loop(shared_steps, blocks, factor_step, carry)
    lax.fori_loop(shared_steps, chunks, panel_only, 0)
    work[total - GROUP:, :] = carry[2]
    hi_w, lo_w = split(jnp.where(lane <= sub, work[...], 0.0).T)
    triple = jnp.concatenate([hi_w, lo_w, hi_w], axis=0)

    def solve_step(c, best):
        base = pl.multiple_of(c * SUB, SUB)
        dots_buf[...] = jnp.dot(
            jnp.concatenate([hi_buf[at(c), :], hi_buf[at(c), :], lo_buf[at(c), :]], axis=1),
            triple, preferred_element_type=f32,
        )
        for p in range(0, SUB, PIECE):
            new_buf[pl.ds(base + p, PIECE), :] = dots_buf[p:p + PIECE, :].astype(bf16)
            squares(lambda j: dots_buf[p:p + PIECE, j:j + LANES], total, p, 0)
        store(c).start()
        sum_buf[:SUB, :LANES] = row_sums(SUB, 0)
        for g in range(SUB // LANES):
            line = jnp.zeros((1, LANES), f32)
            for p in range(g * LANES, (g + 1) * LANES, PIECE):
                line = line + line_part(sum_buf[p:p + PIECE, :LANES], p)
            where = pl.ds(c * (SUB // LANES) + g, 1)
            gain = gain_ref[where, :] - line
            gain_ref[where, :] = gain
            best = jnp.maximum(best, gain)
        return best

    best = lax.fori_loop(0, chunks, solve_step, jnp.full((1, LANES), -jnp.inf, f32))
    best_ref[...] = jnp.broadcast_to(best, best_ref.shape)

    def finish(c, carry):
        store(c).wait()
        return carry

    lax.fori_loop(0, chunks, finish, 0)


def best_kernel(n_rows, n_cols, own_ref, out_ref, buf, send_sem, recv_sem):
    r = lax.axis_index("rows")
    c = lax.axis_index("cols")
    peers = [
        (lax.rem(r + j, n_rows), lax.rem(c + i, n_cols))
        for j in range(n_rows) for i in range(n_cols) if i or j
    ]
    barrier = pltpu.get_barrier_semaphore()
    for peer in peers:
        pl.semaphore_signal(barrier, inc=1, device_id=peer, device_id_type=MESH)
    pl.semaphore_wait(barrier, len(peers))
    copies = []
    for j, peer in enumerate(peers):
        copy = pltpu.make_async_remote_copy(
            src_ref=own_ref, dst_ref=buf.at[j], send_sem=send_sem.at[j],
            recv_sem=recv_sem.at[j], device_id=peer, device_id_type=MESH,
        )
        copy.start()
        copies.append(copy)
    top = own_ref[...]
    for j, copy in enumerate(copies):
        copy.wait_recv()
        top = jnp.maximum(top, buf[j])
    out_ref[0, 0] = jnp.max(top)
    for copy in copies:
        copy.wait_send()


def body(n_rows, n_cols, embeddings, factor_cols, solved, pivots):
    rows_here, width = embeddings.shape
    fac_width = factor_cols.shape[1]
    total = pivots.shape[0]
    devices = n_rows * n_cols
    packet = width + fac_width + LANES
    bf16 = jnp.bfloat16
    vmem = pl.BlockSpec(memory_space=pltpu.VMEM)
    smem = pl.BlockSpec(memory_space=pltpu.SMEM)
    params = functools.partial(pltpu.CompilerParams, vmem_limit_bytes=VMEM_LIMIT)
    own = pl.pallas_call(
        functools.partial(pick_kernel, n_cols),
        out_shape=jax.ShapeDtypeStruct((PMAX, packet), bf16),
        in_specs=[smem, smem, pl.BlockSpec(memory_space=pl.ANY), pl.BlockSpec(memory_space=pl.ANY)],
        out_specs=vmem,
        scratch_shapes=[
            pltpu.VMEM((16 * PMAX, width), bf16),
            pltpu.VMEM((16 * PMAX, fac_width), bf16),
            pltpu.SemaphoreType.DMA((2, PMAX)),
        ],
        compiler_params=params(),
        name="pick",
    )(pivots, solved, embeddings, factor_cols)
    everyone = pl.pallas_call(
        functools.partial(gather_kernel, n_rows, n_cols),
        out_shape=jax.ShapeDtypeStruct((devices, PMAX, packet), bf16),
        in_specs=[vmem],
        out_specs=vmem,
        scratch_shapes=[
            pltpu.SemaphoreType.DMA((devices,)),
            pltpu.SemaphoreType.DMA((devices,)),
            pltpu.SemaphoreType.DMA,
        ],
        compiler_params=params(collective_id=0, has_side_effects=True),
        name="gather",
    )(own)
    lines = rows_here // LANES
    hbm = pl.BlockSpec(memory_space=pl.ANY)
    chunks = rows_here // SUB
    new_cols, gains, best = pl.pallas_call(
        functools.partial(main_kernel, n_cols),
        out_shape=[
            jax.ShapeDtypeStruct((rows_here, total), bf16),
            jax.ShapeDtypeStruct((lines, LANES), jnp.float32),
            jax.ShapeDtypeStruct((8, LANES), jnp.float32),
        ],
        in_specs=[vmem, vmem, vmem, hbm, hbm],
        out_specs=[hbm, vmem, vmem],
        scratch_shapes=[
            pltpu.VMEM((rows_here, width), bf16),
            pltpu.VMEM((rows_here, fac_width), bf16),
            pltpu.VMEM((rows_here, total), bf16),
            pltpu.VMEM((rows_here, total), bf16),
            pltpu.VMEM((rows_here, total), bf16),
            pltpu.VMEM((total, packet), bf16),
            pltpu.VMEM((width + fac_width, total), bf16),
            pltpu.VMEM((total, total), jnp.float32),
            pltpu.VMEM((total, total), jnp.float32),
            pltpu.VMEM((SUB, total), jnp.float32),
            pltpu.VMEM((SUB, total), jnp.float32),
            pltpu.VMEM((SUB, 4 * LANES), bf16),
            pltpu.VMEM((SUB, 3 * LANES), jnp.float32),
            pltpu.SemaphoreType.DMA((2, chunks)),
            pltpu.SemaphoreType.DMA((chunks,)),
        ],
        compiler_params=params(),
        name="main",
    )(
        pivots.reshape(1, total), everyone.reshape(devices * PMAX, packet),
        solved.reshape(lines, LANES), embeddings, factor_cols,
    )
    top = pl.pallas_call(
        functools.partial(best_kernel, n_rows, n_cols),
        out_shape=jax.ShapeDtypeStruct((1, 1), jnp.float32),
        in_specs=[vmem],
        out_specs=smem,
        scratch_shapes=[
            pltpu.VMEM((devices - 1, 8, LANES), jnp.float32),
            pltpu.SemaphoreType.DMA((devices - 1,)),
            pltpu.SemaphoreType.DMA((devices - 1,)),
        ],
        compiler_params=params(collective_id=1, has_side_effects=True),
        name="best",
    )(best)
    return new_cols, gains.reshape(rows_here), top.reshape(())


def solution(mesh):
    n_rows, n_cols = mesh.shape["rows"], mesh.shape["cols"]
    in_specs = (P(("rows", "cols"), None), P(("rows", "cols"), None), P(("rows", "cols")), P())
    out_specs = (P(("rows", "cols"), None), P(("rows", "cols")), P())
    return jax.shard_map(
        functools.partial(body, n_rows, n_cols),
        mesh=mesh, in_specs=in_specs, out_specs=out_specs, check_vma=False,
    )
```

```python
import functools

import jax
import jax.numpy as jnp
from jax import lax
from jax.experimental import pallas as pl
from jax.experimental.pallas import tpu as pltpu
from jax.sharding import PartitionSpec as P

PMAX = 16
EPS = 1e-06
TAU = 6.0
RIDGE = 1.0
LOG2E = 1.4426950408889634
LANES = 128
GROUP = 8
TILE = 1024
SUB = 256
PIECE = 32
VMEM_LIMIT = 56 * 1024 * 1024
MESH = pl.DeviceIdType.MESH
NT = (((1,), (1,)), ((), ()))


def learn(counts):
    c = counts.astype(jnp.float32)
    return (c * (16.0 - c) + 8.0) / 72.0


def pick_kernel(n_cols, piv_ref, solved_ref, emb_ref, fac_ref, out_ref, ebuf, fbuf, sem):
    rows_here, width = emb_ref.shape
    fac_width = fac_ref.shape[1]
    total = piv_ref.shape[0]
    first = (lax.axis_index("rows") * n_cols + lax.axis_index("cols")) * rows_here
    before = jnp.int32(0)
    step = 1
    while step * 2 <= total:
        step *= 2
    while step:
        probe = jnp.minimum(before + step - 1, total - 1)
        inside = before + step <= total
        before = before + jnp.where(inside & (piv_ref[probe] < first), step, 0)
        step //= 2
    copies = []
    spots = []
    for r in range(PMAX):
        idx = jnp.clip(piv_ref[jnp.minimum(before + r, total - 1)] - first, 0, rows_here - 1)
        base = pl.multiple_of(lax.shift_left(lax.shift_right_logical(idx, 4), 4), 16)
        for src, dst, k in ((emb_ref, ebuf, 0), (fac_ref, fbuf, 1)):
            copy = pltpu.make_async_copy(
                src.at[pl.ds(base, 16), :], dst.at[pl.ds(16 * r, 16), :], sem.at[k, r]
            )
            copy.start()
            copies.append(copy)
        spots.append((idx, idx - base + 16 * r))
    row = lax.broadcasted_iota(jnp.int32, (PMAX, 16 * PMAX), 0)
    lane = lax.broadcasted_iota(jnp.int32, (PMAX, 16 * PMAX), 1)
    row1 = lax.broadcasted_iota(jnp.int32, (PMAX, LANES), 0)
    want = jnp.zeros((PMAX, 16 * PMAX), jnp.int32)
    count = jnp.zeros((PMAX, LANES), jnp.int32)
    for r, (idx, spot) in enumerate(spots):
        want = jnp.where(row == r, spot, want)
        count = jnp.where(row1 == r, solved_ref[idx], count)
    pick = jnp.where(lane == want, 1.0, 0.0).astype(jnp.bfloat16)
    out_ref[:, width + fac_width:] = count.astype(jnp.float32).astype(jnp.bfloat16)
    for copy in copies:
        copy.wait()
    out_ref[:, :width] = jnp.dot(
        pick, ebuf[...], preferred_element_type=jnp.float32
    ).astype(jnp.bfloat16)
    out_ref[:, width:width + fac_width] = jnp.dot(
        pick, fbuf[...], preferred_element_type=jnp.float32
    ).astype(jnp.bfloat16)


def gather_kernel(n_rows, n_cols, own_ref, out_ref, send_sem, recv_sem, own_sem):
    r = lax.axis_index("rows")
    c = lax.axis_index("cols")
    pairs = n_cols // 2
    h = c // 2
    k = c - 2 * h
    twin = 2 * h + 1 - k

    def other_row(j):
        return lax.rem(r + j, n_rows)

    def other_col(i):
        return 2 * lax.rem(h + i, pairs) + k

    barrier = pltpu.get_barrier_semaphore()
    peers = [(other_row(j), c) for j in range(1, n_rows)]
    peers += [(r, other_col(i)) for i in range(1, pairs)]
    peers.append((r, twin))
    for peer in peers:
        pl.semaphore_signal(barrier, inc=1, device_id=peer, device_id_type=MESH)
    own = pltpu.make_async_copy(own_ref, out_ref.at[r * n_cols + c], own_sem)
    own.start()
    pl.semaphore_wait(barrier, len(peers))

    sent = []

    def send(src, block, peer):
        copy = pltpu.make_async_remote_copy(
            src_ref=src,
            dst_ref=out_ref.at[block],
            send_sem=send_sem.at[len(sent)],
            recv_sem=recv_sem.at[block],
            device_id=peer,
            device_id_type=MESH,
        )
        copy.start()
        sent.append(copy)

    def arrived(block):
        pltpu.make_async_remote_copy(
            src_ref=own_ref,
            dst_ref=out_ref.at[block],
            send_sem=send_sem.at[0],
            recv_sem=recv_sem.at[block],
            device_id=(r, twin),
            device_id_type=MESH,
        ).wait_recv()

    me = r * n_cols + c
    for i in range(1, pairs):
        send(own_ref, me, (r, other_col(i)))
    for j in range(1, n_rows):
        send(own_ref, me, (other_row(j), c))
    send(own_ref, me, (r, twin))
    order = [j for j in range(1, n_rows)]
    for j in order:
        block = other_row(j) * n_cols + c
        arrived(block)
        for i in range(1, pairs):
            send(out_ref.at[block], block, (r, other_col(i)))
        send(out_ref.at[block], block, (r, twin))
    for j in [0] + order:
        for i in range(1, pairs):
            block = other_row(j) * n_cols + other_col(i)
            arrived(block)
            send(out_ref.at[block], block, (r, twin))
    for j in range(n_rows):
        for i in range(pairs):
            arrived(other_row(j) * n_cols + 2 * lax.rem(h + i, pairs) + 1 - k)
    own.wait()
    for copy in sent:
        copy.wait_send()


def split(x):
    hi = x.astype(jnp.bfloat16)
    return hi, (x - hi.astype(jnp.float32)).astype(jnp.bfloat16)


def factor_kernel(
    rows_here, width, fac_width, piv_ref, all_ref, turn_ref, triple_ref, side_ref, out_ref, work
):
    total = piv_ref.shape[1]
    slots = all_ref.shape[0]
    f32 = jnp.float32
    sub = lax.broadcasted_iota(jnp.int32, (total, total), 0)
    lane = lax.broadcasted_iota(jnp.int32, (total, total), 1)
    eye = sub == lane
    ids = jnp.broadcast_to(piv_ref[...].astype(f32), (total, total))
    ids = jnp.sum(jnp.where(eye, ids, 0.0), axis=1, keepdims=True)
    place = lax.broadcasted_iota(jnp.int32, (total, slots), 0)
    slot = lax.broadcasted_iota(jnp.int32, (total, slots), 1)
    owner = lax.shift_right_logical(slot, PMAX.bit_length() - 1)
    low = (owner * rows_here).astype(f32)
    above = ids >= low
    before = total - jnp.sum(jnp.where(above, 1.0, 0.0), axis=0, keepdims=True)
    rank = place.astype(f32) - before
    chosen = above & (ids < low + rows_here) & (rank == (slot - owner * PMAX).astype(f32))
    chosen = jnp.where(chosen, 1.0, 0.0).astype(jnp.bfloat16)
    full_width = all_ref.shape[1]
    part = width // 2
    for start in range(0, full_width, part):
        size = min(part, full_width - start)
        out_ref[:, start:start + size] = jnp.dot(
            chosen, all_ref[:, start:start + size], preferred_element_type=f32
        ).astype(jnp.bfloat16)
    emb = out_ref[:, :width]
    fac = out_ref[:, width:width + fac_width]
    count = out_ref[:, width + fac_width:width + fac_width + 1].astype(f32)
    wide = emb.astype(f32)
    norm = lax.rsqrt(jnp.sum(wide * wide, axis=1, keepdims=True) / width + EPS)
    q = learn(count)

    def to_row(col):
        return jnp.sum(jnp.where(eye, col, 0.0), axis=0, keepdims=True)

    norm_row = to_row(norm) * (TAU * LOG2E / width)
    q_row = to_row(q)
    side_ref[0:1, :] = norm_row
    side_ref[1:2, :] = q_row
    for start in range(0, width + fac_width, LANES):
        turn_ref[start:start + LANES, :] = (
            out_ref[:, start:start + LANES].astype(f32).T.astype(jnp.bfloat16)
        )
    dots = jnp.dot(emb, turn_ref[:width, :], preferred_element_type=f32)
    shared = jnp.dot(fac, turn_ref[width:, :], preferred_element_type=f32)
    block = q * q_row * jnp.exp2(dots * norm * norm_row - TAU * LOG2E) - shared
    work[...] = block + jnp.where(eye, RIDGE, 0.0)

    row8 = lax.broadcasted_iota(jnp.int32, (GROUP, LANES), 0)
    rows8 = lax.broadcasted_iota(jnp.int32, (GROUP, total), 0)
    lane8 = lax.broadcasted_iota(jnp.int32, (GROUP, total), 1)
    lane_piece = lax.broadcasted_iota(jnp.int32, (PIECE, total), 1)

    def spread(x):
        return jnp.concatenate([x] * (total // LANES), axis=1)

    def thirds(x):
        parts = []
        for _ in range(3):
            part = x.astype(jnp.bfloat16).astype(f32)
            parts.append(part)
            x = x - part
        return parts

    def step(floor, b, carry):
        start = pl.multiple_of(b * GROUP, GROUP)
        rows = work[pl.ds(start, GROUP), :]
        cols = [
            jnp.broadcast_to(
                jnp.sum(jnp.where(lane8 == start + i, rows, 0.0), axis=1, keepdims=True),
                (GROUP, LANES),
            )
            for i in range(GROUP)
        ]
        mine = jnp.where(
            (lane8 >= start) & (lane8 < start + GROUP),
            jnp.where(lane8 == start + rows8, 1.0, 0.0),
            rows,
        )
        diag = jnp.ones((GROUP, LANES), f32)
        for i in range(0, GROUP, 2):
            d0 = cols[i][i:i + 1, :]
            s10 = cols[i][i + 1:i + 2, :]
            det = d0 * cols[i + 1][i + 1:i + 2, :] - s10 * s10
            r0 = 1.0 / d0
            r1 = d0 * (1.0 / det)
            diag = jnp.where(row8 == i, d0, jnp.where(row8 == i + 1, det * r0, diag))
            for j, r in ((i, r0), (i + 1, r1)):
                m = jnp.where(row8 > j, cols[j] * r, 0.0)
                for n in range(j + 1, GROUP):
                    cols[n] = cols[n] - m * cols[n][j:j + 1, :]
                mine = mine - spread(m) * mine[j:j + 1, :]
        mine = mine * spread(lax.rsqrt(diag))
        left = jnp.where(lane8 >= start + GROUP, mine, 0.0)[:, floor:]
        l0, l1, l2 = thirds(left)
        m0, m1, m2 = thirds(mine)
        delta = lax.dot_general(
            jnp.concatenate([l0, l0, l1, l1, l0, l2], axis=0).astype(jnp.bfloat16),
            jnp.concatenate([m0, m1, m0, m1, m2, m0], axis=0).astype(jnp.bfloat16),
            (((0,), (0,)), ((), ())), preferred_element_type=f32,
        )
        gone = (lane_piece >= start) & (lane_piece < start + GROUP)
        for p in range(floor, total, PIECE):
            work[p:p + PIECE, :] = (
                jnp.where(gone, 0.0, work[p:p + PIECE, :]) - delta[p - floor:p - floor + PIECE, :]
            )
        work[pl.ds(start, GROUP), :] = mine
        return carry

    for floor in range(0, total, LANES):
        lax.fori_loop(
            floor // GROUP, (floor + LANES) // GROUP, functools.partial(step, floor), 0
        )
    hi, lo = split(jnp.where(lane <= sub, work[...], 0.0).T)
    triple_ref[:total, :] = hi
    triple_ref[total:2 * total, :] = lo
    triple_ref[2 * total:, :] = hi


def panel_kernel(
    n_cols, rows_here, width,
    emb_ref, fac_ref, solved_ref, ids_ref, turn_ref, triple_ref, side_ref,
    new_ref, gain_ref, best_ref,
    dots_buf, shared_buf, stat_buf, sum_buf, hi_buf, lo_buf,
):
    f32, bf16 = jnp.float32, jnp.bfloat16
    total = ids_ref.shape[1]
    tile = emb_ref.shape[0]
    fac_width = fac_ref.shape[1]
    step = pl.program_id(0)
    first = (lax.axis_index("rows") * n_cols + lax.axis_index("cols")) * rows_here + step * tile
    norm_row = side_ref[0:1, :]
    q_row = side_ref[1:2, :]
    here = ids_ref[...] - first
    small_eye = lax.broadcasted_iota(jnp.int32, (LANES, LANES), 0) == lax.broadcasted_iota(
        jnp.int32, (LANES, LANES), 1
    )
    ones = jnp.ones((2 * LANES, LANES), bf16)
    eye_row = lax.broadcasted_iota(jnp.int32, (PIECE, LANES), 0)
    eye_lane = lax.broadcasted_iota(jnp.int32, (PIECE, LANES), 1)
    row_piece = lax.broadcasted_iota(jnp.int32, (PIECE, total), 0)

    def squares(load, width, p, k):
        acc = jnp.zeros((PIECE, LANES), f32)
        for j in range(0, width, LANES):
            x = load(j).astype(f32)
            acc = acc + x * x
        hi, lo = split(acc)
        stat_buf[p:p + PIECE, k:k + LANES] = hi
        stat_buf[p:p + PIECE, k + LANES:k + 2 * LANES] = lo

    def row_sums(p, rows, k):
        return jnp.dot(stat_buf[p:p + rows, k:k + 2 * LANES], ones, preferred_element_type=f32)

    def line_part(x, p):
        mine = eye_lane == eye_row + p % LANES
        return jnp.sum(jnp.where(mine, x, 0.0), axis=0, keepdims=True)

    dots_buf[...] = jnp.dot(emb_ref[...], turn_ref[:width, :], preferred_element_type=f32)
    shared_buf[...] = jnp.dot(fac_ref[...], turn_ref[width:, :], preferred_element_type=f32)
    for p in range(0, tile, PIECE):
        squares(lambda j: emb_ref[p:p + PIECE, j:j + LANES], width, p, 0)
        squares(lambda j: fac_ref[p:p + PIECE, j:j + LANES], fac_width, p, 2 * LANES)
    sum_buf[:, :LANES] = row_sums(0, tile, 0)
    sum_buf[:, LANES:2 * LANES] = row_sums(0, tile, 2 * LANES)
    for g in range(tile // LANES):
        line = solved_ref[g:g + 1, :].astype(f32)
        counts = jnp.where(small_eye, line, 0.0).astype(bf16)
        sum_buf[g * LANES:(g + 1) * LANES, 2 * LANES:] = jnp.dot(
            counts, ones[:LANES, :], preferred_element_type=f32
        )
    best = jnp.full((1, LANES), -jnp.inf, f32)
    for s in range(0, tile, SUB):
        for p in range(s, s + SUB, PIECE):
            rows = slice(p, p + PIECE)
            norm = lax.rsqrt(sum_buf[rows, :LANES] / width + EPS)
            q = learn(sum_buf[rows, 2 * LANES:])
            for k in range(0, total, LANES):
                half = slice(k, k + LANES)
                power = dots_buf[rows, half] * norm * norm_row[:, half] - TAU * LOG2E
                panel = q * q_row[:, half] * jnp.exp2(power) - shared_buf[rows, half]
                panel = jnp.where(row_piece[:, half] == here[:, half] - p, panel + RIDGE, panel)
                hi, lo = split(panel)
                hi_buf[rows, half] = hi
                lo_buf[rows, half] = lo
        sub = slice(s, s + SUB)
        dots_buf[sub, :] = jnp.dot(
            jnp.concatenate([hi_buf[sub, :], hi_buf[sub, :], lo_buf[sub, :]], axis=1),
            triple_ref[...], preferred_element_type=f32,
        )
        for p in range(s, s + SUB, PIECE):
            new_ref[p:p + PIECE, :] = dots_buf[p:p + PIECE, :].astype(bf16)
            squares(lambda j: dots_buf[p:p + PIECE, j:j + LANES], total, p, 0)
        sum_buf[sub, :LANES] = row_sums(s, SUB, 0)
        for g in range(s // LANES, (s + SUB) // LANES):
            line = jnp.zeros((1, LANES), f32)
            for p in range(g * LANES, (g + 1) * LANES, PIECE):
                rows = slice(p, p + PIECE)
                q = learn(sum_buf[rows, 2 * LANES:])
                line = line + line_part(
                    q * q + RIDGE - sum_buf[rows, LANES:2 * LANES] - sum_buf[rows, :LANES], p
                )
            gain_ref[g:g + 1, :] = line
            best = jnp.maximum(best, line)
    best = jnp.broadcast_to(best, best_ref.shape)

    @pl.when(step == 0)
    def _():
        best_ref[...] = best

    @pl.when(step > 0)
    def _():
        best_ref[...] = jnp.maximum(best_ref[...], best)


def best_kernel(n_rows, n_cols, own_ref, out_ref, stage, buf_r, buf_c, send_r, recv_r, send_c, recv_c):
    r = lax.axis_index("rows")
    c = lax.axis_index("cols")
    barrier = pltpu.get_barrier_semaphore()
    peers_r = [(lax.rem(r + j, n_rows), c) for j in range(1, n_rows)]
    peers_c = [(r, lax.rem(c + i, n_cols)) for i in range(1, n_cols)]
    for peer in peers_r + peers_c:
        pl.semaphore_signal(barrier, inc=1, device_id=peer, device_id_type=MESH)
    pl.semaphore_wait(barrier, len(peers_r) + len(peers_c))

    def exchange(src, buf, send_sem, recv_sem, peers):
        copies = []
        for j, peer in enumerate(peers):
            copy = pltpu.make_async_remote_copy(
                src_ref=src, dst_ref=buf.at[j], send_sem=send_sem.at[j],
                recv_sem=recv_sem.at[j], device_id=peer, device_id_type=MESH,
            )
            copy.start()
            copies.append(copy)
        top = src[...]
        for j, copy in enumerate(copies):
            copy.wait_recv()
            top = jnp.maximum(top, buf[j])
        for copy in copies:
            copy.wait_send()
        return top

    stage[...] = exchange(own_ref, buf_r, send_r, recv_r, peers_r)
    out_ref[0, 0] = jnp.max(exchange(stage, buf_c, send_c, recv_c, peers_c))


def body(n_rows, n_cols, embeddings, factor_cols, solved, pivots):
    rows_here, width = embeddings.shape
    fac_width = factor_cols.shape[1]
    total = pivots.shape[0]
    devices = n_rows * n_cols
    packet = width + fac_width + LANES
    bf16 = jnp.bfloat16
    vmem = pl.BlockSpec(memory_space=pltpu.VMEM)
    smem = pl.BlockSpec(memory_space=pltpu.SMEM)
    params = functools.partial(pltpu.CompilerParams, vmem_limit_bytes=VMEM_LIMIT)
    own = pl.pallas_call(
        functools.partial(pick_kernel, n_cols),
        out_shape=jax.ShapeDtypeStruct((PMAX, packet), bf16),
        in_specs=[smem, smem, pl.BlockSpec(memory_space=pl.ANY), pl.BlockSpec(memory_space=pl.ANY)],
        out_specs=vmem,
        scratch_shapes=[
            pltpu.VMEM((16 * PMAX, width), bf16),
            pltpu.VMEM((16 * PMAX, fac_width), bf16),
            pltpu.SemaphoreType.DMA((2, PMAX)),
        ],
        compiler_params=params(),
        name="pick",
    )(pivots, solved, embeddings, factor_cols)
    everyone = pl.pallas_call(
        functools.partial(gather_kernel, n_rows, n_cols),
        out_shape=jax.ShapeDtypeStruct((devices, PMAX, packet), bf16),
        in_specs=[vmem],
        out_specs=vmem,
        scratch_shapes=[
            pltpu.SemaphoreType.DMA((devices,)),
            pltpu.SemaphoreType.DMA((devices,)),
            pltpu.SemaphoreType.DMA,
        ],
        compiler_params=params(collective_id=0, has_side_effects=True),
        name="gather",
    )(own)
    ids = pivots.reshape(1, total)
    turn, triple, side = pl.pallas_call(
        functools.partial(factor_kernel, rows_here, width, fac_width),
        out_shape=[
            jax.ShapeDtypeStruct((width + fac_width, total), bf16),
            jax.ShapeDtypeStruct((3 * total, total), bf16),
            jax.ShapeDtypeStruct((8, total), jnp.float32),
        ],
        in_specs=[vmem, vmem],
        out_specs=[vmem] * 3,
        scratch_shapes=[
            pltpu.VMEM((total, packet), bf16),
            pltpu.VMEM((total, total), jnp.float32),
        ],
        compiler_params=params(),
        name="factor",
    )(ids, everyone.reshape(devices * PMAX, packet))
    tile = TILE
    lines = rows_here // LANES

    def whole(shape):
        return pl.BlockSpec(shape, lambda t: (0, 0))

    new_cols, gains, best = pl.pallas_call(
        functools.partial(panel_kernel, n_cols, rows_here, width),
        out_shape=[
            jax.ShapeDtypeStruct((rows_here, total), bf16),
            jax.ShapeDtypeStruct((lines, LANES), jnp.float32),
            jax.ShapeDtypeStruct((8, LANES), jnp.float32),
        ],
        grid=(rows_here // tile,),
        in_specs=[
            pl.BlockSpec((tile, width), lambda t: (t, 0)),
            pl.BlockSpec((tile, fac_width), lambda t: (t, 0)),
            pl.BlockSpec((tile // LANES, LANES), lambda t: (t, 0)),
            whole((1, total)),
            whole((width + fac_width, total)),
            whole((3 * total, total)),
            whole((8, total)),
        ],
        out_specs=[
            pl.BlockSpec((tile, total), lambda t: (t, 0)),
            pl.BlockSpec((tile // LANES, LANES), lambda t: (t, 0)),
            whole((8, LANES)),
        ],
        scratch_shapes=[
            pltpu.VMEM((tile, total), jnp.float32),
            pltpu.VMEM((tile, total), jnp.float32),
            pltpu.VMEM((tile, 4 * LANES), bf16),
            pltpu.VMEM((tile, 3 * LANES), jnp.float32),
            pltpu.VMEM((tile, total), bf16),
            pltpu.VMEM((tile, total), bf16),
        ],
        compiler_params=params(),
        name="panel",
    )(embeddings, factor_cols, solved.reshape(lines, LANES), ids, turn, triple, side)
    top = pl.pallas_call(
        functools.partial(best_kernel, n_rows, n_cols),
        out_shape=jax.ShapeDtypeStruct((1, 1), jnp.float32),
        in_specs=[vmem],
        out_specs=smem,
        scratch_shapes=[
            pltpu.VMEM((8, LANES), jnp.float32),
            pltpu.VMEM((n_rows, 8, LANES), jnp.float32),
            pltpu.VMEM((n_cols, 8, LANES), jnp.float32),
            pltpu.SemaphoreType.DMA((n_rows,)),
            pltpu.SemaphoreType.DMA((n_rows,)),
            pltpu.SemaphoreType.DMA((n_cols,)),
            pltpu.SemaphoreType.DMA((n_cols,)),
        ],
        compiler_params=params(collective_id=1, has_side_effects=True),
        name="best",
    )(best)
    return new_cols, gains.reshape(rows_here), top.reshape(())


def solution(mesh):
    n_rows, n_cols = mesh.shape["rows"], mesh.shape["cols"]
    in_specs = (P(("rows", "cols"), None), P(("rows", "cols"), None), P(("rows", "cols")), P())
    out_specs = (P(("rows", "cols"), None), P(("rows", "cols")), P())
    return jax.shard_map(
        functools.partial(body, n_rows, n_cols),
        mesh=mesh, in_specs=in_specs, out_specs=out_specs, check_vma=False,
    )
```

```python
import functools

import jax
import jax.numpy as jnp
from jax import lax
from jax.experimental import pallas as pl
from jax.experimental.pallas import tpu as pltpu
from jax.sharding import PartitionSpec as P

PMAX = 16
EPS = 1e-06
TAU = 6.0
RIDGE = 1.0
LOG2E = 1.4426950408889634
LANES = 128
GROUP = 8
TILE = 1024
SUB = 256
PIECE = 32
VMEM_LIMIT = 56 * 1024 * 1024
MESH = pl.DeviceIdType.MESH


def learn(counts):
    c = counts.astype(jnp.float32)
    return (c * (16.0 - c) + 8.0) / 72.0


def pick_kernel(n_cols, piv_ref, solved_ref, emb_ref, fac_ref, out_ref, ebuf, fbuf, sem):
    rows_here, width = emb_ref.shape
    fac_width = fac_ref.shape[1]
    total = piv_ref.shape[0]
    first = (lax.axis_index("rows") * n_cols + lax.axis_index("cols")) * rows_here
    before = jnp.int32(0)
    step = 1
    while step * 2 <= total:
        step *= 2
    while step:
        probe = jnp.minimum(before + step - 1, total - 1)
        inside = before + step <= total
        before = before + jnp.where(inside & (piv_ref[probe] < first), step, 0)
        step //= 2
    copies = []
    spots = []
    for r in range(PMAX):
        idx = jnp.clip(piv_ref[jnp.minimum(before + r, total - 1)] - first, 0, rows_here - 1)
        base = pl.multiple_of(lax.shift_left(lax.shift_right_logical(idx, 4), 4), 16)
        for src, dst, k in ((emb_ref, ebuf, 0), (fac_ref, fbuf, 1)):
            copy = pltpu.make_async_copy(
                src.at[pl.ds(base, 16), :], dst.at[pl.ds(16 * r, 16), :], sem.at[k, r]
            )
            copy.start()
            copies.append(copy)
        spots.append((idx, idx - base + 16 * r))
    row = lax.broadcasted_iota(jnp.int32, (PMAX, 16 * PMAX), 0)
    lane = lax.broadcasted_iota(jnp.int32, (PMAX, 16 * PMAX), 1)
    row1 = lax.broadcasted_iota(jnp.int32, (PMAX, LANES), 0)
    want = jnp.zeros((PMAX, 16 * PMAX), jnp.int32)
    count = jnp.zeros((PMAX, LANES), jnp.int32)
    for r, (idx, spot) in enumerate(spots):
        want = jnp.where(row == r, spot, want)
        count = jnp.where(row1 == r, solved_ref[idx], count)
    pick = jnp.where(lane == want, 1.0, 0.0).astype(jnp.bfloat16)
    out_ref[:, width + fac_width:] = count.astype(jnp.float32).astype(jnp.bfloat16)
    for copy in copies:
        copy.wait()
    out_ref[:, :width] = jnp.dot(
        pick, ebuf[...], preferred_element_type=jnp.float32
    ).astype(jnp.bfloat16)
    out_ref[:, width:width + fac_width] = jnp.dot(
        pick, fbuf[...], preferred_element_type=jnp.float32
    ).astype(jnp.bfloat16)


def gather_kernel(n_rows, n_cols, own_ref, out_ref, send_sem, recv_sem, own_sem):
    r = lax.axis_index("rows")
    c = lax.axis_index("cols")
    pairs = n_cols // 2
    h = c // 2
    k = c - 2 * h
    twin = 2 * h + 1 - k

    def other_row(j):
        return lax.rem(r + j, n_rows)

    def other_col(i):
        return 2 * lax.rem(h + i, pairs) + k

    barrier = pltpu.get_barrier_semaphore()
    peers = [(other_row(j), c) for j in range(1, n_rows)]
    peers += [(r, other_col(i)) for i in range(1, pairs)]
    peers.append((r, twin))
    for peer in peers:
        pl.semaphore_signal(barrier, inc=1, device_id=peer, device_id_type=MESH)
    own = pltpu.make_async_copy(own_ref, out_ref.at[r * n_cols + c], own_sem)
    own.start()
    pl.semaphore_wait(barrier, len(peers))

    sent = []

    def send(src, block, peer):
        copy = pltpu.make_async_remote_copy(
            src_ref=src,
            dst_ref=out_ref.at[block],
            send_sem=send_sem.at[len(sent)],
            recv_sem=recv_sem.at[block],
            device_id=peer,
            device_id_type=MESH,
        )
        copy.start()
        sent.append(copy)

    def arrived(block):
        pltpu.make_async_remote_copy(
            src_ref=own_ref,
            dst_ref=out_ref.at[block],
            send_sem=send_sem.at[0],
            recv_sem=recv_sem.at[block],
            device_id=(r, twin),
            device_id_type=MESH,
        ).wait_recv()

    me = r * n_cols + c
    for i in range(1, pairs):
        send(own_ref, me, (r, other_col(i)))
    for j in range(1, n_rows):
        send(own_ref, me, (other_row(j), c))
    send(own_ref, me, (r, twin))
    order = [j for j in range(1, n_rows)]
    for j in order:
        block = other_row(j) * n_cols + c
        arrived(block)
        for i in range(1, pairs):
            send(out_ref.at[block], block, (r, other_col(i)))
        send(out_ref.at[block], block, (r, twin))
    for j in [0] + order:
        for i in range(1, pairs):
            block = other_row(j) * n_cols + other_col(i)
            arrived(block)
            send(out_ref.at[block], block, (r, twin))
    for j in range(n_rows):
        for i in range(pairs):
            arrived(other_row(j) * n_cols + 2 * lax.rem(h + i, pairs) + 1 - k)
    own.wait()
    for copy in sent:
        copy.wait_send()


def split(x):
    hi = x.astype(jnp.bfloat16)
    return hi, (x - hi.astype(jnp.float32)).astype(jnp.bfloat16)


def factor_kernel(
    rows_here, width, fac_width, piv_ref, all_ref, turn_ref, triple_ref, side_ref, out_ref, work
):
    total = piv_ref.shape[1]
    slots = all_ref.shape[0]
    f32 = jnp.float32
    sub = lax.broadcasted_iota(jnp.int32, (total, total), 0)
    lane = lax.broadcasted_iota(jnp.int32, (total, total), 1)
    eye = sub == lane
    ids = jnp.broadcast_to(piv_ref[...].astype(f32), (total, total))
    ids = jnp.sum(jnp.where(eye, ids, 0.0), axis=1, keepdims=True)
    place = lax.broadcasted_iota(jnp.int32, (total, slots), 0)
    slot = lax.broadcasted_iota(jnp.int32, (total, slots), 1)
    owner = lax.shift_right_logical(slot, PMAX.bit_length() - 1)
    low = (owner * rows_here).astype(f32)
    above = ids >= low
    before = total - jnp.sum(jnp.where(above, 1.0, 0.0), axis=0, keepdims=True)
    rank = place.astype(f32) - before
    chosen = above & (ids < low + rows_here) & (rank == (slot - owner * PMAX).astype(f32))
    chosen = jnp.where(chosen, 1.0, 0.0).astype(jnp.bfloat16)
    full_width = all_ref.shape[1]
    part = width // 2
    for start in range(0, full_width, part):
        size = min(part, full_width - start)
        out_ref[:, start:start + size] = jnp.dot(
            chosen, all_ref[:, start:start + size], preferred_element_type=f32
        ).astype(jnp.bfloat16)
    emb = out_ref[:, :width]
    fac = out_ref[:, width:width + fac_width]
    count = out_ref[:, width + fac_width:width + fac_width + 1].astype(f32)
    wide = emb.astype(f32)
    norm = lax.rsqrt(jnp.sum(wide * wide, axis=1, keepdims=True) / width + EPS)
    q = learn(count)

    def to_row(col):
        return jnp.sum(jnp.where(eye, col, 0.0), axis=0, keepdims=True)

    norm_row = to_row(norm) * (TAU * LOG2E / width)
    q_row = to_row(q)
    side_ref[0:1, :] = norm_row
    side_ref[1:2, :] = q_row
    for start in range(0, width + fac_width, LANES):
        turn_ref[start:start + LANES, :] = (
            out_ref[:, start:start + LANES].astype(f32).T.astype(jnp.bfloat16)
        )
    dots = jnp.dot(emb, turn_ref[:width, :], preferred_element_type=f32)
    shared = jnp.dot(fac, turn_ref[width:, :], preferred_element_type=f32)
    block = q * q_row * jnp.exp2(dots * norm * norm_row - TAU * LOG2E) - shared
    work[...] = block + jnp.where(eye, RIDGE, 0.0)

    row8 = lax.broadcasted_iota(jnp.int32, (GROUP, LANES), 0)
    rows8 = lax.broadcasted_iota(jnp.int32, (GROUP, total), 0)
    lane8 = lax.broadcasted_iota(jnp.int32, (GROUP, total), 1)
    lane_piece = lax.broadcasted_iota(jnp.int32, (PIECE, total), 1)

    def spread(x):
        return jnp.concatenate([x] * (total // LANES), axis=1)

    def thirds(x):
        parts = []
        for _ in range(3):
            part = x.astype(jnp.bfloat16).astype(f32)
            parts.append(part)
            x = x - part
        return parts

    def step(floor, b, carry):
        start = pl.multiple_of(b * GROUP, GROUP)
        rows = work[pl.ds(start, GROUP), :]
        cols = [
            jnp.broadcast_to(
                jnp.sum(jnp.where(lane8 == start + i, rows, 0.0), axis=1, keepdims=True),
                (GROUP, LANES),
            )
            for i in range(GROUP)
        ]
        mine = jnp.where(
            (lane8 >= start) & (lane8 < start + GROUP),
            jnp.where(lane8 == start + rows8, 1.0, 0.0),
            rows,
        )
        diag = jnp.ones((GROUP, LANES), f32)
        for i in range(0, GROUP, 2):
            d0 = cols[i][i:i + 1, :]
            s10 = cols[i][i + 1:i + 2, :]
            det = d0 * cols[i + 1][i + 1:i + 2, :] - s10 * s10
            r0 = 1.0 / d0
            r1 = d0 * (1.0 / det)
            diag = jnp.where(row8 == i, d0, jnp.where(row8 == i + 1, det * r0, diag))
            for j, r in ((i, r0), (i + 1, r1)):
                m = jnp.where(row8 > j, cols[j] * r, 0.0)
                for n in range(j + 1, GROUP):
                    cols[n] = cols[n] - m * cols[n][j:j + 1, :]
                mine = mine - spread(m) * mine[j:j + 1, :]
        mine = mine * spread(lax.rsqrt(diag))
        left = jnp.where(lane8 >= start + GROUP, mine, 0.0)[:, floor:]
        l0, l1, l2 = thirds(left)
        m0, m1, m2 = thirds(mine)
        delta = lax.dot_general(
            jnp.concatenate([l0, l0, l1, l1, l0, l2], axis=0).astype(jnp.bfloat16),
            jnp.concatenate([m0, m1, m0, m1, m2, m0], axis=0).astype(jnp.bfloat16),
            (((0,), (0,)), ((), ())), preferred_element_type=f32,
        )
        gone = (lane_piece >= start) & (lane_piece < start + GROUP)
        for p in range(floor, total, PIECE):
            work[p:p + PIECE, :] = (
                jnp.where(gone, 0.0, work[p:p + PIECE, :]) - delta[p - floor:p - floor + PIECE, :]
            )
        work[pl.ds(start, GROUP), :] = mine
        return carry

    for floor in range(0, total, LANES):
        lax.fori_loop(
            floor // GROUP, (floor + LANES) // GROUP, functools.partial(step, floor), 0
        )
    hi, lo = split(jnp.where(lane <= sub, work[...], 0.0).T)
    triple_ref[:total, :] = hi
    triple_ref[total:2 * total, :] = lo
    triple_ref[2 * total:, :] = hi


def panel_kernel(
    n_cols, rows_here, width, emb_ref, fac_ref, solved_ref, ids_ref, turn_ref, triple_ref, side_ref,
    new_ref, gain_ref, best_ref,
):
    f32 = jnp.float32
    total = ids_ref.shape[1]
    tile = emb_ref.shape[0]
    step = pl.program_id(0)
    first = (lax.axis_index("rows") * n_cols + lax.axis_index("cols")) * rows_here + step * tile
    norm_row = side_ref[0:1, :]
    q_row = side_ref[1:2, :]
    ids = ids_ref[...] - first
    sub = lax.broadcasted_iota(jnp.int32, (LANES, LANES), 0)
    lane = lax.broadcasted_iota(jnp.int32, (LANES, LANES), 1)
    eye = sub == lane
    row = lax.broadcasted_iota(jnp.int32, (SUB, total), 0)
    q_lanes = learn(solved_ref[...])
    best = jnp.full((1, LANES), -jnp.inf, f32)
    for s in range(0, tile, SUB):
        emb = emb_ref[s:s + SUB, :]
        fac = fac_ref[s:s + SUB, :]
        dots = jnp.dot(emb, turn_ref[:width, :], preferred_element_type=f32)
        shared = jnp.dot(fac, turn_ref[width:, :], preferred_element_type=f32)
        wide = emb.astype(f32)
        norm = lax.rsqrt(jnp.sum(wide * wide, axis=1, keepdims=True) / width + EPS)
        widef = fac.astype(f32)
        used = jnp.sum(widef * widef, axis=1, keepdims=True)
        q = jnp.concatenate(
            [
                jnp.sum(
                    jnp.where(eye, q_lanes[g:g + 1, :], 0.0), axis=1, keepdims=True
                )
                for g in range(s // LANES, (s + SUB) // LANES)
            ],
            axis=0,
        )
        panel = q * q_row * jnp.exp2(dots * norm * norm_row - TAU * LOG2E) - shared
        panel = jnp.where(row + s == ids, panel + RIDGE, panel)
        hi, lo = split(panel)
        full = jnp.dot(
            jnp.concatenate([hi, hi, lo], axis=1), triple_ref[...], preferred_element_type=f32
        )
        new_ref[s:s + SUB, :] = full.astype(jnp.bfloat16)
        gain = q * q + RIDGE - used - jnp.sum(full * full, axis=1, keepdims=True)
        for g in range(0, SUB, LANES):
            line = jnp.sum(jnp.where(eye, gain[g:g + LANES, :], 0.0), axis=0, keepdims=True)
            at = (s + g) // LANES
            gain_ref[at:at + 1, :] = line
            best = jnp.maximum(best, line)
    best = jnp.broadcast_to(best, best_ref.shape)

    @pl.when(step == 0)
    def _():
        best_ref[...] = best

    @pl.when(step > 0)
    def _():
        best_ref[...] = jnp.maximum(best_ref[...], best)


def best_kernel(n_rows, n_cols, own_ref, out_ref, stage, buf_r, buf_c, send_r, recv_r, send_c, recv_c):
    r = lax.axis_index("rows")
    c = lax.axis_index("cols")
    barrier = pltpu.get_barrier_semaphore()
    peers_r = [(lax.rem(r + j, n_rows), c) for j in range(1, n_rows)]
    peers_c = [(r, lax.rem(c + i, n_cols)) for i in range(1, n_cols)]
    for peer in peers_r + peers_c:
        pl.semaphore_signal(barrier, inc=1, device_id=peer, device_id_type=MESH)
    pl.semaphore_wait(barrier, len(peers_r) + len(peers_c))

    def exchange(src, buf, send_sem, recv_sem, peers):
        copies = []
        for j, peer in enumerate(peers):
            copy = pltpu.make_async_remote_copy(
                src_ref=src, dst_ref=buf.at[j], send_sem=send_sem.at[j],
                recv_sem=recv_sem.at[j], device_id=peer, device_id_type=MESH,
            )
            copy.start()
            copies.append(copy)
        top = src[...]
        for j, copy in enumerate(copies):
            copy.wait_recv()
            top = jnp.maximum(top, buf[j])
        for copy in copies:
            copy.wait_send()
        return top

    stage[...] = exchange(own_ref, buf_r, send_r, recv_r, peers_r)
    out_ref[0, 0] = jnp.max(exchange(stage, buf_c, send_c, recv_c, peers_c))


def body(n_rows, n_cols, embeddings, factor_cols, solved, pivots):
    rows_here, width = embeddings.shape
    fac_width = factor_cols.shape[1]
    total = pivots.shape[0]
    devices = n_rows * n_cols
    packet = width + fac_width + LANES
    bf16 = jnp.bfloat16
    vmem = pl.BlockSpec(memory_space=pltpu.VMEM)
    smem = pl.BlockSpec(memory_space=pltpu.SMEM)
    params = functools.partial(pltpu.CompilerParams, vmem_limit_bytes=VMEM_LIMIT)
    own = pl.pallas_call(
        functools.partial(pick_kernel, n_cols),
        out_shape=jax.ShapeDtypeStruct((PMAX, packet), bf16),
        in_specs=[smem, smem, pl.BlockSpec(memory_space=pl.ANY), pl.BlockSpec(memory_space=pl.ANY)],
        out_specs=vmem,
        scratch_shapes=[
            pltpu.VMEM((16 * PMAX, width), bf16),
            pltpu.VMEM((16 * PMAX, fac_width), bf16),
            pltpu.SemaphoreType.DMA((2, PMAX)),
        ],
        compiler_params=params(),
        name="pick",
    )(pivots, solved, embeddings, factor_cols)
    everyone = pl.pallas_call(
        functools.partial(gather_kernel, n_rows, n_cols),
        out_shape=jax.ShapeDtypeStruct((devices, PMAX, packet), bf16),
        in_specs=[vmem],
        out_specs=vmem,
        scratch_shapes=[
            pltpu.SemaphoreType.DMA((devices,)),
            pltpu.SemaphoreType.DMA((devices,)),
            pltpu.SemaphoreType.DMA,
        ],
        compiler_params=params(collective_id=0, has_side_effects=True),
        name="gather",
    )(own)
    ids = pivots.reshape(1, total)
    turn, triple, side = pl.pallas_call(
        functools.partial(factor_kernel, rows_here, width, fac_width),
        out_shape=[
            jax.ShapeDtypeStruct((width + fac_width, total), bf16),
            jax.ShapeDtypeStruct((3 * total, total), bf16),
            jax.ShapeDtypeStruct((8, total), jnp.float32),
        ],
        in_specs=[vmem, vmem],
        out_specs=[vmem] * 3,
        scratch_shapes=[
            pltpu.VMEM((total, packet), bf16),
            pltpu.VMEM((total, total), jnp.float32),
        ],
        compiler_params=params(),
        name="factor",
    )(ids, everyone.reshape(devices * PMAX, packet))
    tile = TILE
    lines = rows_here // LANES

    def whole(shape):
        return pl.BlockSpec(shape, lambda t: (0, 0))

    new_cols, gains, best = pl.pallas_call(
        functools.partial(panel_kernel, n_cols, rows_here, width),
        out_shape=[
            jax.ShapeDtypeStruct((rows_here, total), bf16),
            jax.ShapeDtypeStruct((lines, LANES), jnp.float32),
            jax.ShapeDtypeStruct((8, LANES), jnp.float32),
        ],
        grid=(rows_here // tile,),
        in_specs=[
            pl.BlockSpec((tile, width), lambda t: (t, 0)),
            pl.BlockSpec((tile, fac_width), lambda t: (t, 0)),
            pl.BlockSpec((tile // LANES, LANES), lambda t: (t, 0)),
            whole((1, total)),
            whole((width + fac_width, total)),
            whole((3 * total, total)),
            whole((8, total)),
        ],
        out_specs=[
            pl.BlockSpec((tile, total), lambda t: (t, 0)),
            pl.BlockSpec((tile // LANES, LANES), lambda t: (t, 0)),
            whole((8, LANES)),
        ],
        compiler_params=params(),
        name="panel",
    )(embeddings, factor_cols, solved.reshape(lines, LANES), ids, turn, triple, side)
    top = pl.pallas_call(
        functools.partial(best_kernel, n_rows, n_cols),
        out_shape=jax.ShapeDtypeStruct((1, 1), jnp.float32),
        in_specs=[vmem],
        out_specs=smem,
        scratch_shapes=[
            pltpu.VMEM((8, LANES), jnp.float32),
            pltpu.VMEM((n_rows, 8, LANES), jnp.float32),
            pltpu.VMEM((n_cols, 8, LANES), jnp.float32),
            pltpu.SemaphoreType.DMA((n_rows,)),
            pltpu.SemaphoreType.DMA((n_rows,)),
            pltpu.SemaphoreType.DMA((n_cols,)),
            pltpu.SemaphoreType.DMA((n_cols,)),
        ],
        compiler_params=params(collective_id=1, has_side_effects=True),
        name="best",
    )(best)
    return new_cols, gains.reshape(rows_here), top.reshape(())


def solution(mesh):
    n_rows, n_cols = mesh.shape["rows"], mesh.shape["cols"]
    in_specs = (P(("rows", "cols"), None), P(("rows", "cols"), None), P(("rows", "cols")), P())
    out_specs = (P(("rows", "cols"), None), P(("rows", "cols")), P())
    return jax.shard_map(
        functools.partial(body, n_rows, n_cols),
        mesh=mesh, in_specs=in_specs, out_specs=out_specs, check_vma=False,
    )
```
